32 devices in a mesh: ctx: 8 (over z, y), head: 4 (over x, core).
Axes of the slice: x: 2, y: 2, z: 4, core: 2. Of those that a mesh axis runs over, the one named last changes fastest.
Arguments:
- out_grad: bfloat16 [8192, 2048], P(('ctx', 'head')), may hold values from -6 to 6
- keep_mask: int32 [8192, 2048], P(('ctx', 'head')), may hold values 0 or 1
- out_weight: bfloat16 [2048, 2048], P('head'), may hold values from -0.125 to 0.125
- query_rows: bfloat16 [8192, 2048], P('ctx', 'head'), may hold values from -0.1875 to 0.1875
- key_rows: bfloat16 [8192, 2048], P('ctx', 'head'), may hold values from -0.1875 to 0.1875
- value_rows: bfloat16 [8192, 2048], P('ctx', 'head'), may hold values from -0.1875 to 0.1875
Outputs:
- query_grad: bfloat16 [8192, 2048], P('ctx', 'head')
- key_grad: bfloat16 [8192, 2048], P('ctx', 'head')
- value_grad: bfloat16 [8192, 2048], P('ctx', 'head')
The draws below stay inside these ranges and needn't reach their ends.
All inputs are finite; a program needn't handle non-finite values. No bound on the sum of `keep_mask` on one device may be relied on, other than what follows from the above.
Results may differ from the reference program's by a relative error of at most 0.0065.
Values may be sent and summed in bfloat16 or wider, within the bound.
No kernel may reach another device: no remote copies, remote signals or barrier semaphores. Data moves between devices by JAX's collectives and lax.ppermute only.
A program may use at most 128 MiB of HBM per device.

```python
import jax
import jax.numpy as jnp
from jax import lax

D = 2048
HEADS = 16
HEAD_DIM = 128
TOK_CTX = 1024
SEQ = 8192
N_CTX = 8


def plant(array, rng, smallest, top_value):
    shape = array.shape
    place = [jax.random.randint(jax.random.fold_in(rng, axis), (), 0, shape[axis]) for axis in range(len(shape))]
    array = array.at[tuple(place)].set(smallest)
    longest = shape.index(max(shape))
    place[longest] = (place[longest] + 1) % shape[longest]
    return array.at[tuple(place)].set(top_value)


def shard_levels(own_key, dims, pieces, low, high):
    def one(dim, parts):
        draws = jax.random.uniform(jax.random.fold_in(jax.random.fold_in(own_key, 6), dim), (parts,), jnp.float32, low / len(pieces), high / len(pieces))
        return jnp.repeat(jnp.exp(draws), dims[dim] // parts).reshape((-1,) + (1,) * (len(dims) - dim - 1))

    gain = one(*pieces[0])
    for cut in pieces[1:]:
        gain = gain * one(*cut)
    return gain


def normal_values(stream_key, extent, deviation, most, cuts=(), dtype=jnp.bfloat16):
    result = jax.random.normal(stream_key, extent, jnp.float32) * deviation
    if len(cuts) > 0:
        result = shard_levels(stream_key, extent, cuts, -0.22, 0.18) * result
    return jnp.clip(result, min=-most, max=most).astype(dtype)


def setup_inputs(seed: int = 0) -> dict:
    arg_keys = jax.random.split(jax.random.key(seed), 7)
    out_grad = normal_values(arg_keys[0], (SEQ, D), 1.0, 6.0, ((0, 32),))
    keep_mask = plant((jax.random.randint(arg_keys[1], (SEQ, D), 0, 10) < 9).astype(jnp.int32), jax.random.fold_in(arg_keys[1], 1), 0, 1)
    out_weight = normal_values(arg_keys[2], (D, D), D ** -0.5, 0.125, ((0, 4),))
    query_rows = normal_values(arg_keys[3], (SEQ, D), ((TOK_CTX * N_CTX * HEAD_DIM) ** -0.25), 0.1875, ((0, 8), (1, 4)))
    key_rows = normal_values(arg_keys[4], (SEQ, D), ((TOK_CTX * N_CTX * HEAD_DIM) ** -0.25), 0.1875, ((0, 8), (1, 4)))
    value_rows = normal_values(arg_keys[5], (SEQ, D), ((TOK_CTX * N_CTX * HEAD_DIM) ** -0.25), 0.1875, ((0, 8), (1, 4)))
    return {"out_grad": out_grad, "keep_mask": keep_mask, "out_weight": out_weight, "query_rows": query_rows, "key_rows": key_rows, "value_rows": value_rows}


KEEP_SCALE = 1.0 / 0.9


def split_heads(matrix):
    return matrix.reshape(N_CTX, TOK_CTX, HEADS, HEAD_DIM)


def block_grads(operands):
    query_blk, key_blk, value_blk, grad_blk, state_prev, state_next = operands
    query_float = query_blk.astype(jnp.float32)
    key_float = key_blk.astype(jnp.float32)
    value_float = value_blk.astype(jnp.float32)
    grad_float = grad_blk.astype(jnp.float32)
    row_index = lax.broadcasted_iota(jnp.int32, (TOK_CTX, TOK_CTX), 0)
    column_index = lax.broadcasted_iota(jnp.int32, (TOK_CTX, TOK_CTX), 1)
    causal = row_index >= column_index
    grad_scores = jnp.einsum('thf,shf->hts', grad_float, value_float)
    grad_scores = jnp.where(causal, grad_scores, 0.0).astype(jnp.bfloat16).astype(jnp.float32)
    attn_scores = jnp.einsum('the,she->hts', query_float, key_float)
    attn_scores = jnp.where(causal, attn_scores, 0.0).astype(jnp.bfloat16).astype(jnp.float32)
    prev_round = state_prev.astype(jnp.bfloat16).astype(jnp.float32)
    next_round = state_next.astype(jnp.bfloat16).astype(jnp.float32)
    query_out = jnp.einsum('hts,she->the', grad_scores, key_float) + jnp.einsum('thf,hef->the', grad_float, prev_round)
    key_out = jnp.einsum('hts,the->she', grad_scores, query_float) + jnp.einsum('shf,hef->she', value_float, next_round)
    value_out = jnp.einsum('hts,thf->shf', attn_scores, grad_float) + jnp.einsum('she,hef->shf', key_float, next_round)
    return (query_out.astype(jnp.bfloat16), key_out.astype(jnp.bfloat16), value_out.astype(jnp.bfloat16))


def reference(out_grad, keep_mask, out_weight, query_rows, key_rows, value_rows):
    masked = (out_grad.astype(jnp.float32) * keep_mask.astype(jnp.float32) * KEEP_SCALE).astype(jnp.bfloat16)
    attn_grad = lax.dot_general(masked, out_weight, (((1,), (1,)), ((), ())), preferred_element_type=jnp.float32).astype(jnp.bfloat16)
    query_blocks = split_heads(query_rows)
    key_blocks = split_heads(key_rows)
    value_blocks = split_heads(value_rows)
    grad_blocks = split_heads(attn_grad)
    key_value = jnp.einsum('bthe,bthf->bhef', key_blocks.astype(jnp.float32), value_blocks.astype(jnp.float32))
    query_grad_state = jnp.einsum('bthe,bthf->bhef', query_blocks.astype(jnp.float32), grad_blocks.astype(jnp.float32))
    empty = jnp.zeros((1, HEADS, HEAD_DIM, HEAD_DIM), jnp.float32)
    state_prev = jnp.concatenate([empty, jnp.cumsum(key_value, axis=0)[:-1]], axis=0)
    suffix_incl = jnp.flip(jnp.cumsum(jnp.flip(query_grad_state, 0), axis=0), 0)
    state_next = jnp.concatenate([suffix_incl[1:], empty], axis=0)
    query_out, key_out, value_out = lax.map(block_grads, (query_blocks, key_blocks, value_blocks, grad_blocks, state_prev, state_next))
    return (query_out.reshape(SEQ, D), key_out.reshape(SEQ, D), value_out.reshape(SEQ, D))
```

```python
import functools

import jax
import jax.numpy as jnp
from jax import lax
from jax.experimental import pallas as pl
from jax.experimental.pallas import tpu as pltpu
from jax.sharding import PartitionSpec as P

HEAD_DIM = 128
KEEP_SCALE = 1.0 / 0.9
CHUNKS = 4
SUB = 256
F32 = jnp.float32
BF16 = jnp.bfloat16
NT = (((1,), (1,)), ((), ()))
NN = (((1,), (0,)), ((), ()))
TN = (((0,), (0,)), ((), ()))
MIB = 1024 * 1024


def dot(left, right, dims):
    return lax.dot_general(left, right, dims, preferred_element_type=F32)


def vmem():
    return pl.BlockSpec(memory_space=pltpu.VMEM)


def smem():
    return pl.BlockSpec(memory_space=pltpu.SMEM)


def params(mib):
    return pltpu.CompilerParams(vmem_limit_bytes=mib * MIB)


def cost(flops, nbytes):
    return pl.CostEstimate(flops=flops, bytes_accessed=nbytes, transcendentals=0)


def kv_body(key_ref, value_ref, wide_ref, short_ref):
    for h in range(wide_ref.shape[0]):
        cols = slice(h * HEAD_DIM, (h + 1) * HEAD_DIM)
        state = dot(key_ref[:, cols], value_ref[:, cols], TN)
        wide_ref[h] = state
        short_ref[h] = state.astype(BF16)


def kv_state(key_rows, value_rows):
    tokens, width = key_rows.shape
    heads = width // HEAD_DIM
    shape = (heads, HEAD_DIM, HEAD_DIM)
    return pl.pallas_call(
        kv_body,
        out_shape=(jax.ShapeDtypeStruct(shape, F32), jax.ShapeDtypeStruct(shape, BF16)),
        in_specs=[vmem(), vmem()],
        out_specs=(vmem(), vmem()),
        compiler_params=params(12),
        cost_estimate=cost(2 * tokens * width * HEAD_DIM, 4 * tokens * width),
        name="kv_state",
    )(key_rows, value_rows)


def grad_body(pieces, first, last, own_rows, *refs):
    place_ref, query_ref, weight_ref = refs[:3]
    refs = refs[3:]
    before_ref = None
    if not first:
        before_ref, refs = refs[0], refs[1:]
    masked_refs, refs = refs[: len(pieces)], refs[len(pieces) :]
    grad_ref, state_ref = refs[:2]
    heads = state_ref.shape[0]
    place = place_ref[0]
    sums = [None if first else before_ref[h] for h in range(heads)]
    at = 0
    for ref, (flip, row) in zip(masked_refs, pieces):
        rows = ref.shape[0]
        grad = dot(ref[...], weight_ref[...], NT).astype(BF16)
        grad_ref[at : at + rows, :] = grad
        at += rows
        start = pl.multiple_of(jnp.bitwise_xor(place, flip) * own_rows + row, 16)
        query = query_ref[pl.ds(start, rows), :]
        for h in range(heads):
            cols = slice(h * HEAD_DIM, (h + 1) * HEAD_DIM)
            part = dot(query[:, cols], grad[:, cols], TN)
            sums[h] = part if sums[h] is None else sums[h] + part
    for h in range(heads):
        state_ref[h] = sums[h]
        if last:
            refs[2][h] = sums[h].astype(BF16)


def grad_part(place, query_rows, out_weight, before, pieces, arrays, own_rows, last, name):
    width, model = out_weight.shape
    heads = width // HEAD_DIM
    rows = sum(a.shape[0] for a in arrays)
    shape = (heads, HEAD_DIM, HEAD_DIM)
    out_shape = [jax.ShapeDtypeStruct((rows, width), BF16), jax.ShapeDtypeStruct(shape, F32)]
    if last:
        out_shape.append(jax.ShapeDtypeStruct(shape, BF16))
    first = before is None
    operands = [place, query_rows, out_weight] + ([] if first else [before]) + list(arrays)
    return pl.pallas_call(
        functools.partial(grad_body, pieces, first, last, own_rows),
        out_shape=tuple(out_shape),
        in_specs=[smem()] + [vmem()] * (len(operands) - 1),
        out_specs=tuple(vmem() for _ in out_shape),
        compiler_params=params(20),
        cost_estimate=cost(2 * rows * width * model, 2 * (rows + width) * model),
        name=name,
    )(*operands)


def block_body(places, own_rows, *refs):
    place_ref, query_ref, key_ref, value_ref, prev_ref = refs[:5]
    grad_refs = refs[5 : 5 + len(places)]
    query_out, key_part, value_part, grad = refs[5 + len(places) :]
    place = place_ref[0]
    for ref, pieces in zip(grad_refs, places):
        for at, rows, flip, row in pieces:
            start = pl.multiple_of(jnp.bitwise_xor(place, flip) * own_rows + row, 16)
            grad[pl.ds(start, rows), :] = ref[at : at + rows, :]
    tokens = query_ref.shape[0]
    count = tokens // SUB
    row_id = lax.broadcasted_iota(jnp.int32, (SUB, SUB), 0)
    col_id = lax.broadcasted_iota(jnp.int32, (SUB, SUB), 1)
    prev = prev_ref[0].astype(BF16)
    rows = [slice(i * SUB, (i + 1) * SUB) for i in range(count)]
    for i in range(count):
        g_i, q_i = grad[rows[i], :], query_ref[rows[i], :]
        total = dot(g_i, prev, NT)
        for j in range(i + 1):
            k_j, v_j = key_ref[rows[j], :], value_ref[rows[j], :]
            scores = dot(g_i, v_j, NT)
            scores_t = dot(v_j, g_i, NT)
            attn_t = dot(k_j, q_i, NT)
            if i == j:
                scores = jnp.where(row_id >= col_id, scores, 0.0)
                scores_t = jnp.where(col_id >= row_id, scores_t, 0.0)
                attn_t = jnp.where(col_id >= row_id, attn_t, 0.0)
            total = total + dot(scores.astype(BF16), k_j, NN)
            key_add = dot(scores_t.astype(BF16), q_i, NN)
            value_add = dot(attn_t.astype(BF16), g_i, NN)
            if i == j:
                key_part[rows[j], :] = key_add
                value_part[rows[j], :] = value_add
            else:
                key_part[rows[j], :] += key_add
                value_part[rows[j], :] += value_add
        query_out[rows[i], :] = total.astype(BF16)


def block_products(place, query_rows, key_rows, value_rows, prev, grads, places, own_rows):
    tokens, width = query_rows.shape
    heads = width // HEAD_DIM
    column = lambda rows: pl.BlockSpec((rows, HEAD_DIM), lambda h: (0, h))
    return pl.pallas_call(
        functools.partial(block_body, places, own_rows),
        out_shape=(
            jax.ShapeDtypeStruct((tokens, width), BF16),
            jax.ShapeDtypeStruct((tokens, width), F32),
            jax.ShapeDtypeStruct((tokens, width), F32),
        ),
        grid=(heads,),
        in_specs=[smem()]
        + [column(tokens)] * 3
        + [pl.BlockSpec((1, HEAD_DIM, HEAD_DIM), lambda h: (h, 0, 0))]
        + [column(g.shape[0]) for g in grads],
        out_specs=(column(tokens), column(tokens), column(tokens)),
        scratch_shapes=[pltpu.VMEM((tokens, HEAD_DIM), BF16)],
        compiler_params=params(20),
        cost_estimate=cost(10 * tokens * tokens * width, 20 * tokens * width),
        name="block_products",
    )(place, query_rows, key_rows, value_rows, prev, *grads)


def end_body(key_ref, value_ref, key_part, value_part, next_ref, key_out, value_out):
    state = next_ref[0].astype(BF16)
    key_out[...] = (key_part[...] + dot(value_ref[...], state, NT)).astype(BF16)
    value_out[...] = (value_part[...] + dot(key_ref[...], state, NN)).astype(BF16)


def end_products(key_rows, value_rows, key_part, value_part, state_next):
    tokens, width = key_rows.shape
    heads = width // HEAD_DIM
    column = pl.BlockSpec((tokens, HEAD_DIM), lambda h: (0, h))
    return pl.pallas_call(
        end_body,
        out_shape=(jax.ShapeDtypeStruct((tokens, width), BF16),) * 2,
        grid=(heads,),
        in_specs=[column] * 4 + [pl.BlockSpec((1, HEAD_DIM, HEAD_DIM), lambda h: (h, 0, 0))],
        out_specs=(column, column),
        compiler_params=params(12),
        cost_estimate=cost(4 * tokens * width * HEAD_DIM, 16 * tokens * width),
        name="end_products",
    )(key_rows, value_rows, key_part, value_part, state_next)


def radices(size):
    steps = []
    while size > 1:
        steps.append(2)
        size //= 2
    return steps


def scan_states(own, axis, reverse):
    size, place = lax.axis_size(axis), lax.axis_index(axis)
    total = own
    result = jnp.zeros(own.shape, F32)
    reach = 1
    group = own.astype(F32)
    if size > 1:
        other = lax.ppermute(own, axis, [(i, i ^ 1) for i in range(size)]).astype(F32)
        odd = (place % 2) == 1
        result = jnp.where(odd if not reverse else jnp.logical_not(odd), other, 0.0)
        group = group + other
        reach = 2
    first = True
    carried = group
    while reach < size:
        if reverse:
            pairs = [(i + reach, i) for i in range(size - reach)]
        else:
            pairs = [(i, i + reach) for i in range(size - reach)]
        got = lax.ppermute(carried.astype(BF16), axis, pairs).astype(F32)
        result = result + got
        carried = carried + got
        reach *= 2
    return result


def per_device(out_grad, keep_mask, out_weight, query_rows, key_rows, value_rows):
    size = lax.axis_size("head")
    place = lax.axis_index("head").astype(jnp.int32).reshape(1)
    own_rows = out_grad.shape[0]
    step = own_rows // CHUNKS

    def swap(array, distance):
        return lax.ppermute(array, "head", [(i, i ^ distance) for i in range(size)])

    masked = [
        (
            out_grad[c * step : (c + 1) * step].astype(F32)
            * keep_mask[c * step : (c + 1) * step].astype(F32)
            * KEEP_SCALE
        ).astype(BF16)
        for c in range(CHUNKS)
    ]
    far = [swap(m, 2) for m in masked]
    near = [swap(m, 1) for m in masked]
    both = [swap(m, 1) for m in far]

    kv_wide, kv_short = kv_state(key_rows, value_rows)
    state_prev = scan_states(kv_short, "ctx", False)

    parts = [
        [(0, c, masked[c]) for c in range(CHUNKS)] + [(1, c, near[c]) for c in range(CHUNKS)],
        [(2, c, far[c]) for c in range(CHUNKS - 1)] + [(3, c, both[c]) for c in range(CHUNKS - 1)],
        [(2, CHUNKS - 1, far[-1]), (3, CHUNKS - 1, both[-1])],
    ]
    before, grads, places = None, [], []
    for n, part in enumerate(parts):
        last = n == len(parts) - 1
        got = grad_part(
            place,
            query_rows,
            out_weight,
            before,
            tuple((flip, c * step) for flip, c, _ in part),
            [a for _, _, a in part],
            own_rows,
            last,
            "grad_part_%d" % n,
        )
        grads.append(got[0])
        places.append(tuple((i * step, step, flip, c * step) for i, (flip, c, _) in enumerate(part)))
        before = got[1]
    state_next = scan_states(got[2], "ctx", True)

    query_out, key_part, value_part = block_products(
        place, query_rows, key_rows, value_rows, state_prev, grads, tuple(places), own_rows
    )
    key_out, value_out = end_products(key_rows, value_rows, key_part, value_part, state_next)
    return query_out, key_out, value_out


def solution(mesh):
    placed = (
        P(("ctx", "head"), None),
        P(("ctx", "head"), None),
        P("head", None),
        P("ctx", "head"),
        P("ctx", "head"),
        P("ctx", "head"),
    )
    return jax.shard_map(
        per_device,
        mesh=mesh,
        in_specs=placed,
        out_specs=(P("ctx", "head"), P("ctx", "head"), P("ctx", "head")),
        check_vma=False,
    )
```

```python
import functools

import jax
import jax.numpy as jnp
from jax import lax
from jax.experimental import pallas as pl
from jax.experimental.pallas import tpu as pltpu
from jax.sharding import PartitionSpec as P

HEAD_DIM = 128
KEEP_SCALE = 1.0 / 0.9
F32 = jnp.float32
BF16 = jnp.bfloat16
NT = (((1,), (1,)), ((), ()))
NN = (((1,), (0,)), ((), ()))
TN = (((0,), (0,)), ((), ()))
MIB = 1024 * 1024


def dot(left, right, dims):
    return lax.dot_general(left, right, dims, preferred_element_type=F32)


def vmem():
    return pl.BlockSpec(memory_space=pltpu.VMEM)


def smem():
    return pl.BlockSpec(memory_space=pltpu.SMEM)


def hbm():
    return pl.BlockSpec(memory_space=pltpu.HBM)


def params(mib):
    return pltpu.CompilerParams(vmem_limit_bytes=mib * MIB)


def cost(flops, nbytes):
    return pl.CostEstimate(flops=flops, bytes_accessed=nbytes, transcendentals=0)


def head_cols(h):
    return slice(h * HEAD_DIM, (h + 1) * HEAD_DIM)


def masked_rows(grad, keep):
    return (grad.astype(F32) * keep.astype(F32) * KEEP_SCALE).astype(BF16)


def fetch(source, target, sems, row, rows, pieces):
    size = rows // pieces
    copies = []
    for n in range(pieces):
        copy = pltpu.make_async_copy(
            source.at[pl.ds(row + n * size, size), :],
            target.at[pl.ds(n * size, size), :],
            sems.at[n],
        )
        copy.start()
        copies.append(copy)
    return copies


def mask_body(grad_ref, keep_ref, *refs):
    out_refs, (grad, keep, grad_sems, keep_sems) = refs[:-4], refs[-4:]
    rows = grad.shape[0]
    pieces = keep_sems.shape[0]
    size = rows // pieces
    keep_copies = fetch(keep_ref, keep, keep_sems, 0, rows, pieces)
    grad_copies = fetch(grad_ref, grad, grad_sems, 0, rows, pieces)
    for n in range(pieces):
        keep_copies[n].wait()
        grad_copies[n].wait()
        low, high = n * size, (n + 1) * size
        value = masked_rows(grad[low:high, :], keep[low:high, :])
        out_refs[0][low:high, :] = value
        at = 0
        for ref in out_refs[1:]:
            end = at + ref.shape[0]
            top, bottom = max(low, at), min(high, end)
            if top < bottom:
                ref[top - at : bottom - at, :] = value[top - low : bottom - low, :]
            at = end


def mask_all(out_grad, keep_mask, split):
    rows, model = out_grad.shape
    pieces = 8
    shapes = [rows] + list(split)
    return pl.pallas_call(
        mask_body,
        out_shape=tuple(jax.ShapeDtypeStruct((n, model), BF16) for n in shapes),
        in_specs=[hbm(), hbm()],
        out_specs=(vmem(),) * len(shapes),
        scratch_shapes=[
            pltpu.VMEM((rows, model), BF16),
            pltpu.VMEM((rows, model), jnp.int32),
            pltpu.SemaphoreType.DMA((pieces,)),
            pltpu.SemaphoreType.DMA((pieces,)),
        ],
        compiler_params=params(56),
        cost_estimate=cost(1, 1),
        name="mask_all",
    )(out_grad, keep_mask)


def kv_body(sub, key_ref, value_ref, wide_ref, short_ref, local_ref):
    for h in range(wide_ref.shape[0]):
        total = jnp.zeros(wide_ref.shape[1:], F32)
        for n in range(local_ref.shape[0]):
            local_ref[n, h] = total
            rows = slice(n * sub, (n + 1) * sub)
            total = total + dot(key_ref[rows, head_cols(h)], value_ref[rows, head_cols(h)], TN)
        wide_ref[h] = total
        short_ref[h] = total.astype(BF16)


def kv_state(key_rows, value_rows, sub):
    tokens, width = key_rows.shape
    heads = width // HEAD_DIM
    shape = (heads, HEAD_DIM, HEAD_DIM)
    return pl.pallas_call(
        functools.partial(kv_body, sub),
        out_shape=(
            jax.ShapeDtypeStruct(shape, F32),
            jax.ShapeDtypeStruct(shape, BF16),
            jax.ShapeDtypeStruct((tokens // sub,) + shape, F32),
        ),
        in_specs=[vmem(), vmem()],
        out_specs=(vmem(), vmem(), vmem()),
        compiler_params=params(12),
        cost_estimate=cost(1, 1),
        name="kv_state",
    )(key_rows, value_rows)


def group_body(count, wide_ref, *refs):
    total = wide_ref[...]
    for ref in refs[:count]:
        total = total + ref[...].astype(F32)
    refs[-1][...] = total.astype(BF16)


def after(array, *others):
    return lax.optimization_barrier((array,) + others)[0]


def group_state(wide, received, ties, name):
    received = received[:-1] + [after(received[-1], *ties)]
    return pl.pallas_call(
        functools.partial(group_body, len(received)),
        out_shape=jax.ShapeDtypeStruct(wide.shape, BF16),
        in_specs=[vmem()] * (1 + len(received)),
        out_specs=vmem(),
        compiler_params=params(4),
        cost_estimate=cost(1, 1),
        name=name,
    )(wide, *received)


def grad_body(pieces, sub, befores, last, *refs):
    place_ref, query_ref, weight_ref = refs[:3]
    refs = refs[3:]
    before_refs, refs = refs[:befores], refs[befores:]
    masked_refs, refs = refs[: len(pieces)], refs[len(pieces) :]
    grad_ref, state_ref = refs[:2]
    masked, query = refs[-2:]
    place = place_ref[0]
    spots, at = [], 0
    for ref, (flip, row) in zip(masked_refs, pieces):
        rows = ref.shape[0]
        masked[at : at + rows, :] = ref[...]
        start = pl.multiple_of(jnp.bitwise_xor(place, flip) * sub + row, 16)
        query[at : at + rows, :] = query_ref[pl.ds(start, rows), :]
        spots.append(slice(at, at + rows))
        at += rows
    grad = dot(masked[...], weight_ref[...], NT).astype(BF16)
    grad_ref[...] = grad
    for h in range(state_ref.shape[1]):
        total = None
        for n, rows in enumerate(spots):
            state = dot(query[rows, head_cols(h)], grad[rows, head_cols(h)], TN)
            if last:
                state = state + before_refs[0][n, h]
                other = before_refs[1][n, h]
                total = state + other if total is None else total + (state + other)
            state_ref[n, h] = state
        if last:
            wide_ref, short_ref = refs[2:4]
            wide_ref[h] = total
            short_ref[h] = total.astype(BF16)


def grad_part(place, query_rows, out_weight, sub, befores, pieces, arrays, name):
    width, model = out_weight.shape
    heads = width // HEAD_DIM
    rows = sum(a.shape[0] for a in arrays)
    shape = (heads, HEAD_DIM, HEAD_DIM)
    last = len(befores) > 0
    out_shape = [
        jax.ShapeDtypeStruct((rows, width), BF16),
        jax.ShapeDtypeStruct((len(pieces),) + shape, F32),
    ]
    if last:
        out_shape += [jax.ShapeDtypeStruct(shape, F32), jax.ShapeDtypeStruct(shape, BF16)]
    operands = [place, query_rows, out_weight] + list(befores) + list(arrays)
    return pl.pallas_call(
        functools.partial(grad_body, pieces, sub, len(befores), last),
        out_shape=tuple(out_shape),
        in_specs=[smem()] + [vmem()] * (len(operands) - 1),
        out_specs=tuple(vmem() for _ in out_shape),
        scratch_shapes=[pltpu.VMEM((rows, model), BF16), pltpu.VMEM((rows, width), BF16)],
        compiler_params=params(20),
        cost_estimate=cost(1, 1),
        name=name,
    )(*operands)


def gather_grad(place_ref, grad_refs, places, own_rows, grad):
    place = place_ref[0]
    for ref, pieces in zip(grad_refs, places):
        for at, rows, flip, row in pieces:
            start = pl.multiple_of(jnp.bitwise_xor(place, flip) * own_rows + row, 16)
            grad[pl.ds(start, rows), :] = ref[at : at + rows, :]


def causal(size, turned):
    row_id = lax.broadcasted_iota(jnp.int32, (size, size), 0)
    col_id = lax.broadcasted_iota(jnp.int32, (size, size), 1)
    return col_id >= row_id if turned else row_id >= col_id


def pair_state(ctx_ref, refs, reverse):
    odd = jnp.bitwise_and(ctx_ref[0], 1) == 1
    use = jnp.logical_not(odd) if reverse else odd
    total = None
    for n, ref in enumerate(refs):
        value = ref[0].astype(F32)
        if n == 0:
            value = value * use.astype(F32)
        total = value if total is None else total + value
    return total


def query_body(places, sub, parts, place_ref, ctx_ref, key_ref, value_ref, *refs):
    prev_refs, local_ref, refs = refs[:parts], refs[parts], refs[parts + 1 :]
    grad_refs, (out_ref, grad) = refs[: len(places)], refs[len(places) :]
    gather_grad(place_ref, grad_refs, places, sub, grad)
    prev = pair_state(ctx_ref, prev_refs, False)
    keep = causal(sub, False)
    parts = [slice(n * sub, (n + 1) * sub) for n in range(local_ref.shape[0])]
    scores = [dot(grad[rows, :], value_ref[rows, :], NT) for rows in parts]
    states = [(prev + local_ref[n, 0]).astype(BF16) for n in range(len(parts))]
    totals = [dot(grad[rows, :], state, NT) for rows, state in zip(parts, states)]
    scores = [jnp.where(keep, score, 0.0).astype(BF16) for score in scores]
    for rows, score, total in zip(parts, scores, totals):
        total = total + dot(score, key_ref[rows, :], NN)
        out_ref[rows, :] = total.astype(BF16)


def later_body(places, sub, place_ref, query_ref, key_ref, value_ref, near_ref, far_ref, *refs):
    grad_refs, (key_out, value_out, local_ref, grad) = refs[: len(places)], refs[len(places) :]
    gather_grad(place_ref, grad_refs, places, sub, grad)
    place = place_ref[0]
    states = [near_ref[0, 0], near_ref[1, 0], far_ref[0, 0], far_ref[1, 0]]
    keep = causal(sub, True)
    parts = [slice(n * sub, (n + 1) * sub) for n in range(local_ref.shape[0])]
    masked = lambda scores: [jnp.where(keep, score, 0.0).astype(BF16) for score in scores]
    scores = [dot(value_ref[rows, :], grad[rows, :], NT) for rows in parts]
    attn = [dot(key_ref[rows, :], query_ref[rows, :], NT) for rows in parts]
    scores = masked(scores)
    for rows, score in zip(parts, scores):
        key_out[rows, :] = dot(score, query_ref[rows, :], NN)
    attn = masked(attn)
    for rows, score in zip(parts, attn):
        value_out[rows, :] = dot(score, grad[rows, :], NN)
    for n in range(len(parts)):
        total = None
        for flip, state in enumerate(states):
            part = jnp.where(jnp.bitwise_xor(place, flip) > n, state, 0.0)
            total = part if total is None else total + part
        local_ref[n, 0] = total


def column(rows):
    return pl.BlockSpec((rows, HEAD_DIM), lambda h: (0, h))


def head_state():
    return pl.BlockSpec((1, HEAD_DIM, HEAD_DIM), lambda h: (h, 0, 0))


def local_states(count):
    return pl.BlockSpec((count, 1, HEAD_DIM, HEAD_DIM), lambda h: (0, h, 0, 0))


def query_products(place, ctx, key_rows, value_rows, prevs, local_prev, grads, places, sub):
    tokens, width = key_rows.shape
    return pl.pallas_call(
        functools.partial(query_body, places, sub, len(prevs)),
        out_shape=jax.ShapeDtypeStruct((tokens, width), BF16),
        grid=(width // HEAD_DIM,),
        in_specs=[smem(), smem()]
        + [column(tokens)] * 2
        + [head_state()] * len(prevs)
        + [local_states(local_prev.shape[0])]
        + [column(g.shape[0]) for g in grads],
        out_specs=column(tokens),
        scratch_shapes=[pltpu.VMEM((tokens, HEAD_DIM), BF16)],
        compiler_params=params(16),
        cost_estimate=cost(4 * tokens * tokens * width, 8 * tokens * width),
        name="query_products",
    )(place, ctx, key_rows, value_rows, *prevs, local_prev, *grads)


def later_products(place, query_rows, key_rows, value_rows, near, far, grads, places, sub):
    tokens, width = key_rows.shape
    heads, count = width // HEAD_DIM, tokens // sub
    return pl.pallas_call(
        functools.partial(later_body, places, sub),
        out_shape=(
            jax.ShapeDtypeStruct((tokens, width), F32),
            jax.ShapeDtypeStruct((tokens, width), F32),
            jax.ShapeDtypeStruct((count, heads, HEAD_DIM, HEAD_DIM), F32),
        ),
        grid=(heads,),
        in_specs=[smem()]
        + [column(tokens)] * 3
        + [local_states(near.shape[0]), local_states(far.shape[0])]
        + [column(g.shape[0]) for g in grads],
        out_specs=(column(tokens), column(tokens), local_states(count)),
        scratch_shapes=[pltpu.VMEM((tokens, HEAD_DIM), BF16)],
        compiler_params=params(16),
        cost_estimate=cost(8 * tokens * tokens * width, 10 * tokens * width),
        name="later_products",
    )(place, query_rows, key_rows, value_rows, near, far, *grads)


def end_body(sub, ctx_ref, key_ref, value_ref, key_part, value_part, local_ref, *refs):
    later = pair_state(ctx_ref, refs[:-2], True)
    key_out, value_out = refs[-2:]
    for n in range(local_ref.shape[0]):
        rows = slice(n * sub, (n + 1) * sub)
        state = (later + local_ref[n, 0]).astype(BF16)
        key_out[rows, :] = (key_part[rows, :] + dot(value_ref[rows, :], state, NT)).astype(BF16)
        value_out[rows, :] = (value_part[rows, :] + dot(key_ref[rows, :], state, NN)).astype(BF16)


def end_products(ctx, key_rows, value_rows, key_part, value_part, local_next, nexts, sub):
    tokens, width = key_rows.shape
    return pl.pallas_call(
        functools.partial(end_body, sub),
        out_shape=(jax.ShapeDtypeStruct((tokens, width), BF16),) * 2,
        grid=(width // HEAD_DIM,),
        in_specs=[smem()]
        + [column(tokens)] * 4
        + [local_states(local_next.shape[0])]
        + [head_state()] * len(nexts),
        out_specs=(column(tokens), column(tokens)),
        compiler_params=params(16),
        cost_estimate=cost(4 * tokens * width * HEAD_DIM, 16 * tokens * width),
        name="end_products",
    )(ctx, key_rows, value_rows, key_part, value_part, local_next, *nexts)


def scan_step(payload, axis, reach, reverse):
    size = lax.axis_size(axis)
    if reach == 1:
        pairs = [(i, i ^ 1) for i in range(size)]
    elif reverse:
        pairs = [(i + reach, i) for i in range(size - reach)]
    else:
        pairs = [(i, i + reach) for i in range(size - reach)]
    return lax.ppermute(payload, axis, pairs)


def scan_states(wide, short, axis, reverse, ties, name, between=None):
    received, sents, reach, payload = [], [short], 1, short
    size = lax.axis_size(axis)
    while reach < size:
        if reach > 1:
            step_ties = ties[len(received) - 1 : len(received)]
            if between is not None and reach > 2:
                step_ties = [between(payload)]
                between = None
            payload = group_state(wide, received, step_ties, "%s_%d" % (name, reach))
            sents.append(payload)
        received.append(scan_step(payload, axis, reach, reverse))
        reach *= 2
    if between is not None:
        between(payload)
    return received, sents


def per_device(out_grad, keep_mask, out_weight, query_rows, key_rows, value_rows):
    size = lax.axis_size("head")
    place = lax.axis_index("head").astype(jnp.int32).reshape(1)
    ctx = lax.axis_index("ctx").astype(jnp.int32).reshape(1)
    own_rows = out_grad.shape[0]
    split = 9 * own_rows // 16

    def swap(array, distance):
        return lax.ppermute(array, "head", [(i, i ^ distance) for i in range(size)])

    own, first, last = mask_all(out_grad, keep_mask, (split, own_rows - split))
    near = swap(own, 1)
    far_first, far_last = swap(first, 2), swap(last, 2)
    kv_wide, kv_short, local_prev = kv_state(key_rows, value_rows, own_rows)

    part = functools.partial(grad_part, place, query_rows, out_weight, own_rows)
    grads, places, states = [], [], []

    def run(befores, pieces, arrays, name):
        got = part(befores, pieces, arrays, name)
        at, spots = 0, []
        for (flip, row), array in zip(pieces, arrays):
            spots.append((at, array.shape[0], flip, row))
            at += array.shape[0]
        grads.append(got[0])
        places.append(tuple(spots))
        states.append(got[1])
        return got

    def near_part(sent):
        return run([], ((0, 0), (1, 0)), [own, after(near, sent)], "grad_near")[1]

    prevs, _ = scan_states(kv_wide, kv_short, "ctx", False, [], "prev", near_part)

    far_first = after(far_first, prevs[-1], states[0])
    run([], ((2, 0), (3, 0)), [far_first, swap(far_first, 1)], "grad_far")
    _, far, wide, short = run(
        [states[1], states[0]],
        ((2, split), (3, split)),
        [far_last, swap(far_last, 1)],
        "grad_last",
    )

    query_out = query_products(
        place, ctx, key_rows, value_rows, prevs, local_prev, grads, tuple(places), own_rows
    )
    nexts, _ = scan_states(wide, short, "ctx", True, [query_out], "next")
    key_part, value_part, local_next = later_products(
        place, query_rows, key_rows, value_rows, states[0], far, grads, tuple(places), own_rows
    )
    key_out, value_out = end_products(
        ctx, key_rows, value_rows, key_part, value_part, local_next, nexts, own_rows
    )
    return query_out, key_out, value_out


def solution(mesh):
    placed = (
        P(("ctx", "head"), None),
        P(("ctx", "head"), None),
        P("head", None),
        P("ctx", "head"),
        P("ctx", "head"),
        P("ctx", "head"),
    )
    return jax.shard_map(
        per_device,
        mesh=mesh,
        in_specs=placed,
        out_specs=(P("ctx", "head"), P("ctx", "head"), P("ctx", "head")),
        check_vma=False,
    )
```

```python
import functools

import jax
import jax.numpy as jnp
from jax import lax
from jax.experimental import pallas as pl
from jax.experimental.pallas import tpu as pltpu
from jax.sharding import PartitionSpec as P

HEAD_DIM = 128
KEEP_SCALE = 1.0 / 0.9
F32 = jnp.float32
BF16 = jnp.bfloat16
NT = (((1,), (1,)), ((), ()))
NN = (((1,), (0,)), ((), ()))
TN = (((0,), (0,)), ((), ()))
MIB = 1024 * 1024


def dot(left, right, dims):
    return lax.dot_general(left, right, dims, preferred_element_type=F32)


def vmem():
    return pl.BlockSpec(memory_space=pltpu.VMEM)


def smem():
    return pl.BlockSpec(memory_space=pltpu.SMEM)


def hbm():
    return pl.BlockSpec(memory_space=pltpu.HBM)


def params(mib):
    return pltpu.CompilerParams(vmem_limit_bytes=mib * MIB)


def cost(flops, nbytes):
    return pl.CostEstimate(flops=flops, bytes_accessed=nbytes, transcendentals=0)


def head_cols(h):
    return slice(h * HEAD_DIM, (h + 1) * HEAD_DIM)


def masked_rows(grad, keep):
    return (grad.astype(F32) * keep.astype(F32) * KEEP_SCALE).astype(BF16)


def fetch(source, target, sems, row, rows, pieces):
    size = rows // pieces
    copies = []
    for n in range(pieces):
        copy = pltpu.make_async_copy(
            source.at[pl.ds(row + n * size, size), :],
            target.at[pl.ds(n * size, size), :],
            sems.at[n],
        )
        copy.start()
        copies.append(copy)
    return copies


def mask_body(row, grad_ref, keep_ref, *refs):
    out_refs, (grad, keep, grad_sems, keep_sems) = refs[:-4], refs[-4:]
    rows = grad.shape[0]
    pieces = keep_sems.shape[0]
    size = rows // pieces
    keep_copies = fetch(keep_ref, keep, keep_sems, row, rows, pieces)
    grad_copies = fetch(grad_ref, grad, grad_sems, row, rows, pieces)
    for n in range(pieces):
        keep_copies[n].wait()
        grad_copies[n].wait()
        low, high = n * size, (n + 1) * size
        value = masked_rows(grad[low:high, :], keep[low:high, :])
        out_refs[0][low:high, :] = value
        at = 0
        for ref in out_refs[1:]:
            end = at + ref.shape[0]
            top, bottom = max(low, at), min(high, end)
            if top < bottom:
                ref[top - at : bottom - at, :] = value[top - low : bottom - low, :]
            at = end


def mask_rows(out_grad, keep_mask, row, split, name):
    model = out_grad.shape[1]
    rows = sum(split)
    pieces = rows // 16
    return pl.pallas_call(
        functools.partial(mask_body, row),
        out_shape=tuple(jax.ShapeDtypeStruct((n, model), BF16) for n in [rows] + list(split)),
        in_specs=[hbm(), hbm()],
        out_specs=(vmem(),) * (1 + len(split)),
        scratch_shapes=[
            pltpu.VMEM((rows, model), BF16),
            pltpu.VMEM((rows, model), jnp.int32),
            pltpu.SemaphoreType.DMA((pieces,)),
            pltpu.SemaphoreType.DMA((pieces,)),
        ],
        compiler_params=params(56),
        cost_estimate=cost(1, 1),
        name=name,
    )(out_grad, keep_mask)


def kv_body(key_ref, value_ref, wide_ref, short_ref):
    for h in range(wide_ref.shape[0]):
        total = dot(key_ref[:, head_cols(h)], value_ref[:, head_cols(h)], TN)
        wide_ref[h] = total
        short_ref[h] = total.astype(BF16)


def kv_state(key_rows, value_rows):
    heads = key_rows.shape[1] // HEAD_DIM
    shape = (heads, HEAD_DIM, HEAD_DIM)
    return pl.pallas_call(
        kv_body,
        out_shape=(jax.ShapeDtypeStruct(shape, F32), jax.ShapeDtypeStruct(shape, BF16)),
        in_specs=[vmem(), vmem()],
        out_specs=(vmem(), vmem()),
        compiler_params=params(12),
        cost_estimate=cost(1, 1),
        name="kv_state",
    )(key_rows, value_rows)


def group_body(count, wide_ref, *refs):
    total = wide_ref[...]
    for ref in refs[:count]:
        total = total + ref[...].astype(F32)
    refs[-1][...] = total.astype(BF16)


def after(array, *others):
    return lax.optimization_barrier((array,) + others)[0]


def group_state(wide, received, ties, name):
    received = received[:-1] + [after(received[-1], *ties)]
    return pl.pallas_call(
        functools.partial(group_body, len(received)),
        out_shape=jax.ShapeDtypeStruct(wide.shape, BF16),
        in_specs=[vmem()] * (1 + len(received)),
        out_specs=vmem(),
        compiler_params=params(4),
        cost_estimate=cost(1, 1),
        name=name,
    )(wide, *received)


def swap_body(count, ctx_ref, half_ref, prev_ref, wide_ref, *refs):
    total = wide_ref[...]
    for ref in refs[:count]:
        total = total + ref[...].astype(F32)
    upper = ctx_ref[0] >= half_ref[0]
    refs[-1][...] = jnp.where(upper, total, prev_ref[...].astype(F32)).astype(BF16)


def swap_state(ctx, half, prev, wide, received):
    return pl.pallas_call(
        functools.partial(swap_body, len(received)),
        out_shape=jax.ShapeDtypeStruct(wide.shape, BF16),
        in_specs=[smem(), smem()] + [vmem()] * (2 + len(received)),
        out_specs=vmem(),
        compiler_params=params(4),
        cost_estimate=cost(1, 1),
        name="swap_state",
    )(ctx, half, prev, wide, *received)


def grad_body(pieces, sub, befores, last, *refs):
    place_ref, query_ref, weight_ref = refs[:3]
    refs = refs[3:]
    before_refs, refs = refs[:befores], refs[befores:]
    masked_refs, refs = refs[: len(pieces)], refs[len(pieces) :]
    grad_ref, state_ref = refs[:2]
    masked, query = refs[-2:]
    place = place_ref[0]
    spots, at = [], 0
    for ref, (flip, row) in zip(masked_refs, pieces):
        rows = ref.shape[0]
        masked[at : at + rows, :] = ref[...]
        start = pl.multiple_of(jnp.bitwise_xor(place, flip) * sub + row, 16)
        query[at : at + rows, :] = query_ref[pl.ds(start, rows), :]
        if spots and spots[-1][0] == flip:
            spots[-1][2] = at + rows
        else:
            spots.append([flip, at, at + rows])
        at += rows
    spots = [slice(low, high) for _, low, high in spots]
    grad = dot(masked[...], weight_ref[...], NT).astype(BF16)
    grad_ref[...] = grad
    for h in range(state_ref.shape[1]):
        total = None
        for n, rows in enumerate(spots):
            state = dot(query[rows, head_cols(h)], grad[rows, head_cols(h)], TN)
            if last:
                state = state + before_refs[0][n, h]
                other = before_refs[1][n, h]
                total = state + other if total is None else total + (state + other)
            state_ref[n, h] = state
        if last:
            wide_ref, short_ref = refs[2:4]
            wide_ref[h] = total
            short_ref[h] = total.astype(BF16)


def grad_part(place, query_rows, out_weight, sub, befores, pieces, arrays, name):
    width, model = out_weight.shape
    heads = width // HEAD_DIM
    rows = sum(a.shape[0] for a in arrays)
    shape = (heads, HEAD_DIM, HEAD_DIM)
    last = len(befores) > 0
    out_shape = [
        jax.ShapeDtypeStruct((rows, width), BF16),
        jax.ShapeDtypeStruct((2,) + shape, F32),
    ]
    if last:
        out_shape += [jax.ShapeDtypeStruct(shape, F32), jax.ShapeDtypeStruct(shape, BF16)]
    operands = [place, query_rows, out_weight] + list(befores) + list(arrays)
    return pl.pallas_call(
        functools.partial(grad_body, pieces, sub, len(befores), last),
        out_shape=tuple(out_shape),
        in_specs=[smem()] + [vmem()] * (len(operands) - 1),
        out_specs=tuple(vmem() for _ in out_shape),
        scratch_shapes=[pltpu.VMEM((rows, model), BF16), pltpu.VMEM((rows, width), BF16)],
        compiler_params=params(20),
        cost_estimate=cost(1, 1),
        name=name,
    )(*operands)


def gather_grad(place_ref, grad_refs, places, own_rows, grad):
    place = place_ref[0]
    for ref, pieces in zip(grad_refs, places):
        for at, rows, flip, row in pieces:
            start = pl.multiple_of(jnp.bitwise_xor(place, flip) * own_rows + row, 16)
            grad[pl.ds(start, rows), :] = ref[at : at + rows, :]


def causal(size, turned):
    row_id = lax.broadcasted_iota(jnp.int32, (size, size), 0)
    col_id = lax.broadcasted_iota(jnp.int32, (size, size), 1)
    return col_id >= row_id if turned else row_id >= col_id


def pair_state(ctx_ref, refs, reverse):
    odd = jnp.bitwise_and(ctx_ref[0], 1) == 1
    use = jnp.logical_not(odd) if reverse else odd
    total = None
    for n, ref in enumerate(refs):
        value = ref[0].astype(F32)
        if n == 0:
            value = value * use.astype(F32)
        total = value if total is None else total + value
    return total


def query_body(places, sub, parts, place_ref, ctx_ref, key_ref, value_ref, *refs):
    prev_refs, refs = refs[:parts], refs[parts:]
    grad_refs, (out_ref, grad) = refs[: len(places)], refs[len(places) :]
    gather_grad(place_ref, grad_refs, places, sub, grad)
    keep = causal(sub, False)
    rows = [slice(at, at + sub) for at in range(0, key_ref.shape[0], sub)]
    scores = [dot(grad[at, :], value_ref[at, :], NT) for at in rows]
    states = [pair_state(ctx_ref, prev_refs, False)]
    for at in rows[:-1]:
        states.append(states[-1] + dot(key_ref[at, :], value_ref[at, :], TN))
    totals = [dot(grad[at, :], state.astype(BF16), NT) for at, state in zip(rows, states)]
    scores = [jnp.where(keep, score, 0.0).astype(BF16) for score in scores]
    for at, score, total in zip(rows, scores, totals):
        out_ref[at, :] = total + dot(score, key_ref[at, :], NN)


def later_body(places, sub, parts, place_ref, ctx_ref, query_ref, key_ref, value_ref, *refs):
    near_ref, far_ref = refs[:2]
    next_refs, refs = refs[2 : 2 + parts], refs[2 + parts :]
    grad_refs, (key_out, value_out, grad_out, grad) = refs[: len(places)], refs[len(places) :]
    gather_grad(place_ref, grad_refs, places, sub, grad)
    grad_out[...] = grad[...]
    place = place_ref[0]
    keep = causal(sub, True)
    rows = [slice(at, at + sub) for at in range(0, key_ref.shape[0], sub)]
    masked = lambda scores: [jnp.where(keep, score, 0.0).astype(BF16) for score in scores]
    scores = [dot(value_ref[at, :], grad[at, :], NT) for at in rows]
    attn = [dot(key_ref[at, :], query_ref[at, :], NT) for at in rows]
    later = pair_state(ctx_ref, next_refs, True)
    own = [near_ref[0, 0], near_ref[1, 0], far_ref[0, 0], far_ref[1, 0]]
    states = []
    for n in range(len(rows)):
        total = later
        for flip, state in enumerate(own):
            total = total + jnp.where(jnp.bitwise_xor(place, flip) > n, state, 0.0)
        states.append(total.astype(BF16))
    scores = masked(scores)
    for at, score, state in zip(rows, scores, states):
        key_out[at, :] = dot(value_ref[at, :], state, NT) + dot(score, query_ref[at, :], NN)
    attn = masked(attn)
    for at, score, state in zip(rows, attn, states):
        value_out[at, :] = dot(key_ref[at, :], state, NN) + dot(score, grad[at, :], NN)


def column(rows):
    return pl.BlockSpec((rows, HEAD_DIM), lambda h: (0, h))


def head_state():
    return pl.BlockSpec((1, HEAD_DIM, HEAD_DIM), lambda h: (h, 0, 0))


def local_states(count):
    return pl.BlockSpec((count, 1, HEAD_DIM, HEAD_DIM), lambda h: (0, h, 0, 0))


def query_products(place, ctx, key_rows, value_rows, prevs, grads, places, sub):
    tokens, width = key_rows.shape
    return pl.pallas_call(
        functools.partial(query_body, places, sub, len(prevs)),
        out_shape=jax.ShapeDtypeStruct((tokens, width), F32),
        grid=(width // HEAD_DIM,),
        in_specs=[smem(), smem()]
        + [column(tokens)] * 2
        + [head_state()] * len(prevs)
        + [column(g.shape[0]) for g in grads],
        out_specs=column(tokens),
        scratch_shapes=[pltpu.VMEM((tokens, HEAD_DIM), BF16)],
        compiler_params=params(16),
        cost_estimate=cost(4 * tokens * tokens * width, 8 * tokens * width),
        name="query_products",
    )(place, ctx, key_rows, value_rows, *prevs, *grads)


def later_products(place, ctx, query_rows, key_rows, value_rows, near, far, nexts, grads, places, sub):
    tokens, width = key_rows.shape
    return pl.pallas_call(
        functools.partial(later_body, places, sub, len(nexts)),
        out_shape=(
            jax.ShapeDtypeStruct((tokens, width), F32),
            jax.ShapeDtypeStruct((tokens, width), F32),
            jax.ShapeDtypeStruct((tokens, width), BF16),
        ),
        grid=(width // HEAD_DIM,),
        in_specs=[smem(), smem()]
        + [column(tokens)] * 3
        + [local_states(2), local_states(2)]
        + [head_state()] * len(nexts)
        + [column(g.shape[0]) for g in grads],
        out_specs=(column(tokens),) * 3,
        scratch_shapes=[pltpu.VMEM((tokens, HEAD_DIM), BF16)],
        compiler_params=params(16),
        cost_estimate=cost(8 * tokens * tokens * width, 10 * tokens * width),
        name="later_products",
    )(place, ctx, query_rows, key_rows, value_rows, near, far, *nexts, *grads)


def end_body(sub, ctx_ref, half_ref, got_ref, key_ref, value_ref, grad_ref, *refs):
    part_refs, out_refs, (done, sems) = refs[:3], refs[3:6], refs[6:]
    upper = ctx_ref[0] >= half_ref[0]
    heads = got_ref.shape[0]
    copies = []
    for n in range(key_ref.shape[0] // sub):
        rows = slice(n * sub, (n + 1) * sub)
        for h in range(heads):
            cols = head_cols(h)
            got = got_ref[h].astype(F32)
            down = jnp.where(upper, 0.0, got).astype(BF16)
            up = jnp.where(upper, got, 0.0).astype(BF16)
            adds = (
                dot(grad_ref[rows, cols], up, NT),
                dot(value_ref[rows, cols], down, NT),
                dot(key_ref[rows, cols], down, NN),
            )
            for k in range(3):
                done[k, rows, cols] = (part_refs[k][rows, cols] + adds[k]).astype(BF16)
        for k in range(3):
            copy = pltpu.make_async_copy(
                done.at[k, pl.ds(n * sub, sub), :],
                out_refs[k].at[pl.ds(n * sub, sub), :],
                sems.at[k, n],
            )
            copy.start()
            copies.append(copy)
    for copy in copies:
        copy.wait()


def end_products(ctx, half, got, key_rows, value_rows, grad_rows, parts, sub):
    tokens, width = key_rows.shape
    return pl.pallas_call(
        functools.partial(end_body, sub),
        out_shape=(jax.ShapeDtypeStruct((tokens, width), BF16),) * 3,
        in_specs=[smem(), smem()] + [vmem()] * 7,
        out_specs=(hbm(),) * 3,
        scratch_shapes=[
            pltpu.VMEM((3, tokens, width), BF16),
            pltpu.SemaphoreType.DMA((3, tokens // sub)),
        ],
        compiler_params=params(16),
        cost_estimate=cost(6 * tokens * width * HEAD_DIM, 16 * tokens * width),
        name="end_products",
    )(ctx, half, got, key_rows, value_rows, grad_rows, *parts)


def exchange(payload, reach, reverse):
    size = lax.axis_size("ctx")
    if reach == 1:
        pairs = [(i, i ^ 1) for i in range(size)]
    elif reverse:
        pairs = [(i + reach, i) for i in range(size - reach)]
    else:
        pairs = [(i, i + reach) for i in range(size - reach)]
    return lax.ppermute(payload, "ctx", pairs)


def scan_states(wide, short, reverse, tie, name):
    received, reach, payload = [], 1, short
    while reach < lax.axis_size("ctx") // 2:
        if reach > 1:
            payload = group_state(wide, received, [tie] if reach == 2 else [], "%s_%d" % (name, reach))
        received.append(exchange(payload, reach, reverse))
        reach *= 2
    return received


def per_device(out_grad, keep_mask, out_weight, query_rows, key_rows, value_rows):
    size = lax.axis_size("head")
    place = lax.axis_index("head").astype(jnp.int32).reshape(1)
    ctx = lax.axis_index("ctx").astype(jnp.int32).reshape(1)
    own_rows = out_grad.shape[0]
    half = jnp.full((1,), lax.axis_size("ctx") // 2, jnp.int32)
    unit = own_rows // 16
    split = 9 * unit

    def swap(array, distance):
        return lax.ppermute(array, "head", [(i, i ^ distance) for i in range(size)])

    first, *near_first = mask_rows(out_grad, keep_mask, 0, (5 * unit, 4 * unit), "mask_first")
    last, *near_last = mask_rows(out_grad, keep_mask, split, (4 * unit, 3 * unit), "mask_last")
    far_first, far_last = swap(first, 2), swap(last, 2)
    near = [swap(piece, 1) for piece in near_first + near_last]
    kv_wide, kv_short = kv_state(key_rows, value_rows)

    part = functools.partial(grad_part, place, query_rows, out_weight, own_rows)
    grads, places, states = [], [], []

    def run(befores, pieces, arrays, name):
        got = part(befores, pieces, arrays, name)
        at, spots = 0, []
        for (flip, row), array in zip(pieces, arrays):
            spots.append((at, array.shape[0], flip, row))
            at += array.shape[0]
        grads.append(got[0])
        places.append(tuple(spots))
        states.append(got[1])
        return got

    pieces = ((0, 0), (0, split), (1, 0), (1, 5 * unit), (1, split), (1, split + 4 * unit))
    run([], pieces, [first, last] + near[:-1] + [after(near[-1], kv_short)], "grad_near")

    prevs = scan_states(kv_wide, kv_short, False, states[0], "prev")
    prev_sum = group_state(kv_wide, prevs, [], "prev_sum")

    far_first = after(far_first, prev_sum, states[0])
    run([], ((2, 0), (3, 0)), [far_first, swap(far_first, 1)], "grad_far")
    _, far, wide, short = run(
        [states[1], states[0]],
        ((2, split), (3, split)),
        [far_last, swap(far_last, 1)],
        "grad_last",
    )

    spots = tuple(places)
    query_part = query_products(place, ctx, key_rows, value_rows, prevs, grads, spots, own_rows)
    nexts = scan_states(wide, short, True, query_part, "next")
    payload = swap_state(ctx, half, prev_sum, wide, nexts)
    size = lax.axis_size("ctx")
    got = lax.ppermute(payload, "ctx", [(i, (i + size // 2) % size) for i in range(size)])
    key_part, value_part, grad_rows = later_products(
        place, ctx, query_rows, key_rows, value_rows, states[0], far, nexts, grads, spots, own_rows
    )
    parts = (query_part, key_part, value_part)
    return end_products(ctx, half, got, key_rows, value_rows, grad_rows, parts, own_rows)


def solution(mesh):
    placed = (
        P(("ctx", "head"), None),
        P(("ctx", "head"), None),
        P("head", None),
        P("ctx", "head"),
        P("ctx", "head"),
        P("ctx", "head"),
    )
    return jax.shard_map(
        per_device,
        mesh=mesh,
        in_specs=placed,
        out_specs=(P("ctx", "head"), P("ctx", "head"), P("ctx", "head")),
        check_vma=False,
    )
```

```python
import functools

import jax
import jax.numpy as jnp
from jax import lax
from jax.experimental import pallas as pl
from jax.experimental.pallas import tpu as pltpu
from jax.sharding import PartitionSpec as P

HEAD_DIM = 128
QUAD = 4
KEEP_SCALE = 1.0 / 0.9
F32 = jnp.float32
BF16 = jnp.bfloat16
NT = (((1,), (1,)), ((), ()))
NN = (((1,), (0,)), ((), ()))
TN = (((0,), (0,)), ((), ()))
MIB = 1024 * 1024


def dot(left, right, dims):
    return lax.dot_general(left, right, dims, preferred_element_type=F32)


def vmem():
    return pl.BlockSpec(memory_space=pltpu.VMEM)


def smem():
    return pl.BlockSpec(memory_space=pltpu.SMEM)


def hbm():
    return pl.BlockSpec(memory_space=pltpu.HBM)


def params(mib):
    return pltpu.CompilerParams(vmem_limit_bytes=mib * MIB)


def cost(flops, nbytes):
    return pl.CostEstimate(flops=flops, bytes_accessed=nbytes, transcendentals=0)


def head_cols(h):
    return slice(h * HEAD_DIM, (h + 1) * HEAD_DIM)


def masked_rows(grad, keep):
    return (grad.astype(F32) * keep.astype(F32) * KEEP_SCALE).astype(BF16)


def fetch(source, target, sems, row, rows, pieces):
    size = rows // pieces
    copies = []
    for n in range(pieces):
        copy = pltpu.make_async_copy(
            source.at[pl.ds(row + n * size, size), :],
            target.at[pl.ds(n * size, size), :],
            sems.at[n],
        )
        copy.start()
        copies.append(copy)
    return copies


def mask_body(row, grad_ref, keep_ref, *refs):
    out_refs, (grad, keep, grad_sems, keep_sems) = refs[:-4], refs[-4:]
    rows = grad.shape[0]
    pieces = keep_sems.shape[0]
    size = rows // pieces
    keep_copies = fetch(keep_ref, keep, keep_sems, row, rows, pieces)
    grad_copies = fetch(grad_ref, grad, grad_sems, row, rows, pieces)
    for n in range(pieces):
        keep_copies[n].wait()
        grad_copies[n].wait()
        low, high = n * size, (n + 1) * size
        value = masked_rows(grad[low:high, :], keep[low:high, :])
        out_refs[0][low:high, :] = value
        at = 0
        for ref in out_refs[1:]:
            end = at + ref.shape[0]
            top, bottom = max(low, at), min(high, end)
            if top < bottom:
                ref[top - at : bottom - at, :] = value[top - low : bottom - low, :]
            at = end


def mask_rows(out_grad, keep_mask, row, split, name):
    model = out_grad.shape[1]
    rows = sum(split)
    pieces = rows // 16
    return pl.pallas_call(
        functools.partial(mask_body, row),
        out_shape=tuple(jax.ShapeDtypeStruct((n, model), BF16) for n in [rows] + list(split)),
        in_specs=[hbm(), hbm()],
        out_specs=(vmem(),) * (1 + len(split)),
        scratch_shapes=[
            pltpu.VMEM((rows, model), BF16),
            pltpu.VMEM((rows, model), jnp.int32),
            pltpu.SemaphoreType.DMA((pieces,)),
            pltpu.SemaphoreType.DMA((pieces,)),
        ],
        compiler_params=params(56),
        cost_estimate=cost(1, 1),
        name=name,
    )(out_grad, keep_mask)


def kv_body(key_ref, value_ref, wide_ref, short_ref):
    for h in range(wide_ref.shape[0]):
        total = dot(key_ref[:, head_cols(h)], value_ref[:, head_cols(h)], TN)
        wide_ref[h] = total
        short_ref[h] = total.astype(BF16)


def kv_state(key_rows, value_rows):
    heads = key_rows.shape[1] // HEAD_DIM
    shape = (heads, HEAD_DIM, HEAD_DIM)
    return pl.pallas_call(
        kv_body,
        out_shape=(jax.ShapeDtypeStruct(shape, F32), jax.ShapeDtypeStruct(shape, BF16)),
        in_specs=[vmem(), vmem()],
        out_specs=(vmem(), vmem()),
        compiler_params=params(12),
        cost_estimate=cost(1, 1),
        name="kv_state",
    )(key_rows, value_rows)


def group_body(count, wide_ref, *refs):
    total = wide_ref[...]
    for ref in refs[:count]:
        total = total + ref[...].astype(F32)
    refs[-1][...] = total.astype(BF16)


def after(array, *others):
    return lax.optimization_barrier((array,) + others)[0]


def group_state(wide, received, ties, name):
    received = received[:-1] + [after(received[-1], *ties)]
    return pl.pallas_call(
        functools.partial(group_body, len(received)),
        out_shape=jax.ShapeDtypeStruct(wide.shape, BF16),
        in_specs=[vmem()] * (1 + len(received)),
        out_specs=vmem(),
        compiler_params=params(4),
        cost_estimate=cost(1, 1),
        name=name,
    )(wide, *received)


def swap_body(count, ctx_ref, half_ref, prev_ref, wide_ref, *refs):
    total = wide_ref[...]
    for ref in refs[:count]:
        total = total + ref[...].astype(F32)
    upper = ctx_ref[0] >= half_ref[0]
    refs[-1][...] = jnp.where(upper, total, prev_ref[...].astype(F32)).astype(BF16)


def swap_state(ctx, half, prev, wide, received):
    return pl.pallas_call(
        functools.partial(swap_body, len(received)),
        out_shape=jax.ShapeDtypeStruct(wide.shape, BF16),
        in_specs=[smem(), smem()] + [vmem()] * (2 + len(received)),
        out_specs=vmem(),
        compiler_params=params(4),
        cost_estimate=cost(1, 1),
        name="swap_state",
    )(ctx, half, prev, wide, *received)


def grad_body(pieces, sub, befores, last, *refs):
    place_ref, query_ref, weight_ref = refs[:3]
    refs = refs[3:]
    before_refs, refs = refs[:befores], refs[befores:]
    masked_refs, refs = refs[: len(pieces)], refs[len(pieces) :]
    grad_ref, state_ref = refs[:2]
    masked, query, sems = refs[-3:]
    copies = []
    place = place_ref[0]
    spots, at = [], 0
    for ref, (flip, row) in zip(masked_refs, pieces):
        rows = ref.shape[0]
        copy = pltpu.make_async_copy(ref, masked.at[pl.ds(at, rows), :], sems.at[len(copies)])
        copy.start()
        copies.append(copy)
        start = pl.multiple_of(jnp.bitwise_xor(place, flip) * sub + row, 16)
        query[at : at + rows, :] = query_ref[pl.ds(start, rows), :]
        if spots and spots[-1][0] == flip:
            spots[-1][2] = at + rows
        else:
            spots.append([flip, at, at + rows])
        at += rows
    spots = [slice(low, high) for _, low, high in spots]
    for copy in copies:
        copy.wait()
    grad = dot(masked[...], weight_ref[...], NT).astype(BF16)
    grad_ref[...] = grad
    for h in range(state_ref.shape[1]):
        total = None
        for n, rows in enumerate(spots):
            state = dot(query[rows, head_cols(h)], grad[rows, head_cols(h)], TN)
            if last:
                state = state + before_refs[0][n, h]
                other = before_refs[1][n, h]
                total = state + other if total is None else total + (state + other)
            state_ref[n, h] = state
        if last:
            wide_ref, short_ref = refs[2:4]
            wide_ref[h] = total
            short_ref[h] = total.astype(BF16)


def grad_part(place, query_rows, out_weight, sub, befores, pieces, arrays, name, mib=20):
    width, model = out_weight.shape
    heads = width // HEAD_DIM
    rows = sum(a.shape[0] for a in arrays)
    shape = (heads, HEAD_DIM, HEAD_DIM)
    last = len(befores) > 0
    out_shape = [
        jax.ShapeDtypeStruct((rows, width), BF16),
        jax.ShapeDtypeStruct((2,) + shape, F32),
    ]
    if last:
        out_shape += [jax.ShapeDtypeStruct(shape, F32), jax.ShapeDtypeStruct(shape, BF16)]
    operands = [place, query_rows, out_weight] + list(befores) + list(arrays)
    return pl.pallas_call(
        functools.partial(grad_body, pieces, sub, len(befores), last),
        out_shape=tuple(out_shape),
        in_specs=[smem()] + [vmem()] * (2 + len(befores)) + [hbm()] * len(arrays),
        out_specs=tuple(vmem() for _ in out_shape),
        scratch_shapes=[
            pltpu.VMEM((rows, model), BF16),
            pltpu.VMEM((rows, width), BF16),
            pltpu.SemaphoreType.DMA((len(arrays),)),
        ],
        compiler_params=params(mib),
        cost_estimate=cost(1, 1),
        name=name,
    )(*operands)


def gather_grad(place_ref, grad_refs, places, own_rows, grad):
    place = place_ref[0]
    for ref, pieces in zip(grad_refs, places):
        for at, rows, flip, row in pieces:
            start = pl.multiple_of(jnp.bitwise_xor(place, flip) * own_rows + row, 16)
            grad[pl.ds(start, rows), :] = ref[at : at + rows, :]


def causal(size, turned):
    row_id = lax.broadcasted_iota(jnp.int32, (size, size), 0)
    col_id = lax.broadcasted_iota(jnp.int32, (size, size), 1)
    return col_id >= row_id if turned else row_id >= col_id


def near_state(ctx_ref, refs, h, reverse):
    total = None
    for n, ref in enumerate(refs):
        value = ref[h].astype(F32)
        if n < QUAD - 1:
            low = jnp.bitwise_and(ctx_ref[0], 1 if n == 0 else 2) == 0
            value = jnp.where(low if reverse else jnp.logical_not(low), value, 0.0)
        total = value if total is None else total + value
    return total


def query_body(places, sub, parts, place_ref, ctx_ref, key_ref, value_ref, *refs):
    prev_refs, refs = refs[:parts], refs[parts:]
    grad_refs, (out_ref, grad) = refs[: len(places)], refs[len(places) :]
    gather_grad(place_ref, grad_refs, places, sub, grad)
    keep = causal(sub, False)
    rows = [slice(at, at + sub) for at in range(0, key_ref.shape[0], sub)]
    for h in range(key_ref.shape[1] // HEAD_DIM):
        cols = head_cols(h)
        scores = [dot(grad[at, cols], value_ref[at, cols], NT) for at in rows]
        states = [near_state(ctx_ref, prev_refs, h, False)]
        for at in rows[:-1]:
            states.append(states[-1] + dot(key_ref[at, cols], value_ref[at, cols], TN))
        totals = [dot(grad[at, cols], state.astype(BF16), NT) for at, state in zip(rows, states)]
        scores = [jnp.where(keep, score, 0.0).astype(BF16) for score in scores]
        for at, score, total in zip(rows, scores, totals):
            out_ref[at, cols] = total + dot(score, key_ref[at, cols], NN)


def later_body(sub, parts, place_ref, ctx_ref, query_ref, key_ref, value_ref, grad, *refs):
    near_ref, far_ref = refs[:2]
    next_refs, (key_out, value_out) = refs[2 : 2 + parts], refs[2 + parts :]
    place = place_ref[0]
    keep = causal(sub, True)
    rows = [slice(at, at + sub) for at in range(0, key_ref.shape[0], sub)]
    masked = lambda scores: [jnp.where(keep, score, 0.0).astype(BF16) for score in scores]
    for h in range(key_ref.shape[1] // HEAD_DIM):
        cols = head_cols(h)
        scores = [dot(value_ref[at, cols], grad[at, cols], NT) for at in rows]
        attn = [dot(key_ref[at, cols], query_ref[at, cols], NT) for at in rows]
        later = near_state(ctx_ref, next_refs, h, True)
        own = [near_ref[0, h], near_ref[1, h], far_ref[0, h], far_ref[1, h]]
        states = []
        for n in range(len(rows)):
            total = later
            for flip, state in enumerate(own):
                total = total + jnp.where(jnp.bitwise_xor(place, flip) > n, state, 0.0)
            states.append(total.astype(BF16))
        scores = masked(scores)
        for at, score, state in zip(rows, scores, states):
            key_out[at, cols] = dot(value_ref[at, cols], state, NT) + dot(score, query_ref[at, cols], NN)
        attn = masked(attn)
        for at, score, state in zip(rows, attn, states):
            value_out[at, cols] = dot(key_ref[at, cols], state, NN) + dot(score, grad[at, cols], NN)


def query_products(place, ctx, key_rows, value_rows, prevs, grads, places, sub):
    tokens, width = key_rows.shape
    return pl.pallas_call(
        functools.partial(query_body, places, sub, len(prevs)),
        out_shape=(
            jax.ShapeDtypeStruct((tokens, width), F32),
            jax.ShapeDtypeStruct((tokens, width), BF16),
        ),
        in_specs=[smem(), smem()] + [vmem()] * (2 + len(prevs) + len(grads)),
        out_specs=(vmem(), vmem()),
        compiler_params=params(16),
        cost_estimate=cost(4 * tokens * tokens * width, 8 * tokens * width),
        name="query_products",
    )(place, ctx, key_rows, value_rows, *prevs, *grads)


def later_products(place, ctx, query_rows, key_rows, value_rows, grad_rows, near, far, nexts, sub):
    tokens, width = key_rows.shape
    return pl.pallas_call(
        functools.partial(later_body, sub, len(nexts)),
        out_shape=(jax.ShapeDtypeStruct((tokens, width), F32),) * 2,
        in_specs=[smem(), smem()] + [vmem()] * (6 + len(nexts)),
        out_specs=(vmem(), vmem()),
        compiler_params=params(16),
        cost_estimate=cost(8 * tokens * tokens * width, 10 * tokens * width),
        name="later_products",
    )(place, ctx, query_rows, key_rows, value_rows, grad_rows, near, far, *nexts)


def end_body(sub, ctx_ref, half_ref, got_ref, key_ref, value_ref, grad_ref, *refs):
    part_refs, out_refs, (done, sems) = refs[:3], refs[3:6], refs[6:]
    upper = ctx_ref[0] >= half_ref[0]
    heads = got_ref.shape[0]
    copies = []
    for n in range(key_ref.shape[0] // sub):
        rows = slice(n * sub, (n + 1) * sub)
        for h in range(heads):
            cols = head_cols(h)
            got = got_ref[h].astype(F32)
            down = jnp.where(upper, 0.0, got).astype(BF16)
            up = jnp.where(upper, got, 0.0).astype(BF16)
            adds = (
                dot(grad_ref[rows, cols], up, NT),
                dot(value_ref[rows, cols], down, NT),
                dot(key_ref[rows, cols], down, NN),
            )
            for k in range(3):
                done[k, rows, cols] = (part_refs[k][rows, cols] + adds[k]).astype(BF16)
        for k in range(3):
            copy = pltpu.make_async_copy(
                done.at[k, pl.ds(n * sub, sub), :],
                out_refs[k].at[pl.ds(n * sub, sub), :],
                sems.at[k, n],
            )
            copy.start()
            copies.append(copy)
    for copy in copies:
        copy.wait()


def end_products(ctx, half, got, key_rows, value_rows, grad_rows, parts, sub):
    tokens, width = key_rows.shape
    return pl.pallas_call(
        functools.partial(end_body, sub),
        out_shape=(jax.ShapeDtypeStruct((tokens, width), BF16),) * 3,
        in_specs=[smem(), smem()] + [vmem()] * 7,
        out_specs=(hbm(),) * 3,
        scratch_shapes=[
            pltpu.VMEM((3, tokens, width), BF16),
            pltpu.SemaphoreType.DMA((3, tokens // sub)),
        ],
        compiler_params=params(16),
        cost_estimate=cost(6 * tokens * width * HEAD_DIM, 16 * tokens * width),
        name="end_products",
    )(ctx, half, got, key_rows, value_rows, grad_rows, *parts)


def scan_states(wide, short, reverse, ties, name):
    size = lax.axis_size("ctx")
    send = lambda payload, pairs: lax.ppermute(payload, "ctx", pairs)
    received = [send(short, [(i, i ^ k) for i in range(size)]) for k in range(1, QUAD)]
    reach = QUAD
    while reach < size // 2:
        payload = group_state(wide, received, ties if reach == QUAD else [], "%s_%d" % (name, reach))
        if reverse:
            pairs = [(i + reach, i) for i in range(size - reach)]
        else:
            pairs = [(i, i + reach) for i in range(size - reach)]
        received.append(send(payload, pairs))
        reach *= 2
    return received


def per_device(out_grad, keep_mask, out_weight, query_rows, key_rows, value_rows):
    size = lax.axis_size("head")
    place = lax.axis_index("head").astype(jnp.int32).reshape(1)
    ctx = lax.axis_index("ctx").astype(jnp.int32).reshape(1)
    own_rows = out_grad.shape[0]
    half = jnp.full((1,), lax.axis_size("ctx") // 2, jnp.int32)
    unit = own_rows // 16
    split = 9 * unit

    def swap(array, distance):
        return lax.ppermute(array, "head", [(i, i ^ distance) for i in range(size)])

    first, *near_first = mask_rows(out_grad, keep_mask, 0, (5 * unit, 4 * unit), "mask_first")
    last, *near_last = mask_rows(out_grad, keep_mask, split, (4 * unit, 3 * unit), "mask_last")
    far_first, far_last = swap(first, 2), swap(last, 2)
    kv_wide, kv_short = kv_state(key_rows, value_rows)
    prevs = scan_states(kv_wide, kv_short, False, [], "prev")
    near = [swap(piece, 1) for piece in near_first + near_last]

    part = functools.partial(grad_part, place, query_rows, out_weight, own_rows)
    grads, places, states = [], [], []

    def run(befores, pieces, arrays, name, mib=20):
        got = part(befores, pieces, arrays, name, mib)
        at, spots = 0, []
        for (flip, row), array in zip(pieces, arrays):
            spots.append((at, array.shape[0], flip, row))
            at += array.shape[0]
        grads.append(got[0])
        places.append(tuple(spots))
        states.append(got[1])
        return got

    pieces = ((0, 0), (0, split), (1, 0), (1, 5 * unit), (1, split), (1, split + 4 * unit))
    run([], pieces, [first, last] + near, "grad_near", 60)

    prev_sum = group_state(kv_wide, prevs, [states[0]], "prev_sum")

    far_first = after(far_first, prev_sum, states[0])
    run([], ((2, 0), (3, 0)), [far_first, swap(far_first, 1)], "grad_far")
    _, far, wide, short = run(
        [states[1], states[0]],
        ((2, split), (3, split)),
        [far_last, swap(far_last, 1)],
        "grad_last",
    )

    spots = tuple(places)
    query_part, grad_rows = query_products(place, ctx, key_rows, value_rows, prevs, grads, spots, own_rows)
    nexts = scan_states(wide, short, True, [query_part], "next")
    nexts[-1] = after(nexts[-1], query_part)
    payload = swap_state(ctx, half, prev_sum, wide, nexts)
    size = lax.axis_size("ctx")
    got = lax.ppermute(payload, "ctx", [(i, (i + size // 2) % size) for i in range(size)])
    key_part, value_part = later_products(
        place, ctx, query_rows, key_rows, value_rows, grad_rows, states[0], far, nexts, own_rows
    )
    parts = (query_part, key_part, value_part)
    return end_products(ctx, half, got, key_rows, value_rows, grad_rows, parts, own_rows)


def solution(mesh):
    placed = (
        P(("ctx", "head"), None),
        P(("ctx", "head"), None),
        P("head", None),
        P("ctx", "head"),
        P("ctx", "head"),
        P("ctx", "head"),
    )
    return jax.shard_map(
        per_device,
        mesh=mesh,
        in_specs=placed,
        out_specs=(P("ctx", "head"), P("ctx", "head"), P("ctx", "head")),
        check_vma=False,
    )
```

```python
import functools

import jax
import jax.numpy as jnp
from jax import lax
from jax.experimental import pallas as pl
from jax.experimental.pallas import tpu as pltpu
from jax.sharding import PartitionSpec as P

HEAD_DIM = 128
QUAD = 4
KEEP_SCALE = 1.0 / 0.9
F32 = jnp.float32
BF16 = jnp.bfloat16
NT = (((1,), (1,)), ((), ()))
NN = (((1,), (0,)), ((), ()))
TN = (((0,), (0,)), ((), ()))
MIB = 1024 * 1024


def dot(left, right, dims):
    return lax.dot_general(left, right, dims, preferred_element_type=F32)


def vmem():
    return pl.BlockSpec(memory_space=pltpu.VMEM)


def smem():
    return pl.BlockSpec(memory_space=pltpu.SMEM)


def hbm():
    return pl.BlockSpec(memory_space=pltpu.HBM)


def params(mib):
    return pltpu.CompilerParams(vmem_limit_bytes=mib * MIB)


def cost(flops, nbytes):
    return pl.CostEstimate(flops=flops, bytes_accessed=nbytes, transcendentals=0)


def head_cols(h):
    return slice(h * HEAD_DIM, (h + 1) * HEAD_DIM)


def masked_rows(grad, keep):
    return (grad.astype(F32) * keep.astype(F32) * KEEP_SCALE).astype(BF16)


def fetch(source, target, sems, row, rows, pieces):
    size = rows // pieces
    copies = []
    for n in range(pieces):
        copy = pltpu.make_async_copy(
            source.at[pl.ds(row + n * size, size), :],
            target.at[pl.ds(n * size, size), :],
            sems.at[n],
        )
        copy.start()
        copies.append(copy)
    return copies


def mask_body(row, grad_ref, keep_ref, *refs):
    out_refs, (grad, keep, grad_sems, keep_sems) = refs[:-4], refs[-4:]
    rows = grad.shape[0]
    pieces = keep_sems.shape[0]
    size = rows // pieces
    keep_copies = fetch(keep_ref, keep, keep_sems, row, rows, pieces)
    grad_copies = fetch(grad_ref, grad, grad_sems, row, rows, pieces)
    for n in range(pieces):
        keep_copies[n].wait()
        grad_copies[n].wait()
        low, high = n * size, (n + 1) * size
        value = masked_rows(grad[low:high, :], keep[low:high, :])
        out_refs[0][low:high, :] = value
        at = 0
        for ref in out_refs[1:]:
            end = at + ref.shape[0]
            top, bottom = max(low, at), min(high, end)
            if top < bottom:
                ref[top - at : bottom - at, :] = value[top - low : bottom - low, :]
            at = end


def mask_rows(out_grad, keep_mask, row, split, name):
    model = out_grad.shape[1]
    rows = sum(split)
    pieces = rows // 16 if rows % 48 else rows // 48
    return pl.pallas_call(
        functools.partial(mask_body, row),
        out_shape=tuple(jax.ShapeDtypeStruct((n, model), BF16) for n in [rows] + list(split)),
        in_specs=[hbm(), hbm()],
        out_specs=(vmem(),) * (1 + len(split)),
        scratch_shapes=[
            pltpu.VMEM((rows, model), BF16),
            pltpu.VMEM((rows, model), jnp.int32),
            pltpu.SemaphoreType.DMA((pieces,)),
            pltpu.SemaphoreType.DMA((pieces,)),
        ],
        compiler_params=params(56),
        cost_estimate=cost(1, 1),
        name=name,
    )(out_grad, keep_mask)


def kv_body(key_ref, value_ref, wide_ref, short_ref):
    for h in range(wide_ref.shape[0]):
        total = dot(key_ref[:, head_cols(h)], value_ref[:, head_cols(h)], TN)
        wide_ref[h] = total
        short_ref[h] = total.astype(BF16)


def kv_state(key_rows, value_rows):
    heads = key_rows.shape[1] // HEAD_DIM
    shape = (heads, HEAD_DIM, HEAD_DIM)
    return pl.pallas_call(
        kv_body,
        out_shape=(jax.ShapeDtypeStruct(shape, F32), jax.ShapeDtypeStruct(shape, BF16)),
        in_specs=[vmem(), vmem()],
        out_specs=(vmem(), vmem()),
        compiler_params=params(12),
        cost_estimate=cost(1, 1),
        name="kv_state",
    )(key_rows, value_rows)


def group_body(count, wide_ref, *refs):
    total = wide_ref[...]
    for ref in refs[:count]:
        total = total + ref[...].astype(F32)
    refs[-1][...] = total.astype(BF16)


def after(array, *others):
    return lax.optimization_barrier((array,) + others)[0]


def group_state(wide, received, ties, name):
    received = received[:-1] + [after(received[-1], *ties)]
    return pl.pallas_call(
        functools.partial(group_body, len(received)),
        out_shape=jax.ShapeDtypeStruct(wide.shape, BF16),
        in_specs=[vmem()] * (1 + len(received)),
        out_specs=vmem(),
        compiler_params=params(4),
        cost_estimate=cost(1, 1),
        name=name,
    )(wide, *received)


def swap_body(count, ctx_ref, half_ref, prev_ref, wide_ref, *refs):
    total = wide_ref[...]
    for ref in refs[:count]:
        total = total + ref[...].astype(F32)
    upper = ctx_ref[0] >= half_ref[0]
    refs[-1][...] = jnp.where(upper, total, prev_ref[...].astype(F32)).astype(BF16)


def swap_state(ctx, half, prev, wide, received):
    return pl.pallas_call(
        functools.partial(swap_body, len(received)),
        out_shape=jax.ShapeDtypeStruct(wide.shape, BF16),
        in_specs=[smem(), smem()] + [vmem()] * (2 + len(received)),
        out_specs=vmem(),
        compiler_params=params(4),
        cost_estimate=cost(1, 1),
        name="swap_state",
    )(ctx, half, prev, wide, *received)


def grad_body(pieces, sub, befores, last, *refs):
    place_ref, query_ref, weight_ref = refs[:3]
    refs = refs[3:]
    before_refs, refs = refs[:befores], refs[befores:]
    masked_refs, refs = refs[: len(pieces)], refs[len(pieces) :]
    grad_ref, state_ref = refs[:2]
    masked, query, sems = refs[-3:]
    copies = []
    place = place_ref[0]
    spots, at = [], 0
    for ref, (flip, row) in zip(masked_refs, pieces):
        rows = ref.shape[0]
        copy = pltpu.make_async_copy(ref, masked.at[pl.ds(at, rows), :], sems.at[len(copies)])
        copy.start()
        copies.append(copy)
        start = pl.multiple_of(jnp.bitwise_xor(place, flip) * sub + row, 16)
        query[at : at + rows, :] = query_ref[pl.ds(start, rows), :]
        if spots and spots[-1][0] == flip:
            spots[-1][2] = at + rows
        else:
            spots.append([flip, at, at + rows])
        at += rows
    spots = [slice(low, high) for _, low, high in spots]
    for copy in copies:
        copy.wait()
    grad = dot(masked[...], weight_ref[...], NT).astype(BF16)
    grad_ref[...] = grad
    for h in range(state_ref.shape[1]):
        total = None
        for n, rows in enumerate(spots):
            state = dot(query[rows, head_cols(h)], grad[rows, head_cols(h)], TN)
            if last:
                state = state + before_refs[0][n, h]
                other = before_refs[1][n, h]
                total = state + other if total is None else total + (state + other)
            state_ref[n, h] = state
        if last:
            wide_ref, short_ref = refs[2:4]
            wide_ref[h] = total
            short_ref[h] = total.astype(BF16)


def grad_part(place, query_rows, out_weight, sub, befores, pieces, arrays, name, mib=20):
    width, model = out_weight.shape
    heads = width // HEAD_DIM
    rows = sum(a.shape[0] for a in arrays)
    shape = (heads, HEAD_DIM, HEAD_DIM)
    last = len(befores) > 0
    out_shape = [
        jax.ShapeDtypeStruct((rows, width), BF16),
        jax.ShapeDtypeStruct((2,) + shape, F32),
    ]
    if last:
        out_shape += [jax.ShapeDtypeStruct(shape, F32), jax.ShapeDtypeStruct(shape, BF16)]
    operands = [place, query_rows, out_weight] + list(befores) + list(arrays)
    return pl.pallas_call(
        functools.partial(grad_body, pieces, sub, len(befores), last),
        out_shape=tuple(out_shape),
        in_specs=[smem()] + [vmem()] * (2 + len(befores)) + [hbm()] * len(arrays),
        out_specs=tuple(vmem() for _ in out_shape),
        scratch_shapes=[
            pltpu.VMEM((rows, model), BF16),
            pltpu.VMEM((rows, width), BF16),
            pltpu.SemaphoreType.DMA((len(arrays),)),
        ],
        compiler_params=params(mib),
        cost_estimate=cost(1, 1),
        name=name,
    )(*operands)


def gather_grad(place_ref, grad_refs, places, own_rows, grad):
    place = place_ref[0]
    for ref, pieces in zip(grad_refs, places):
        for at, rows, flip, row in pieces:
            start = pl.multiple_of(jnp.bitwise_xor(place, flip) * own_rows + row, 16)
            grad[pl.ds(start, rows), :] = ref[at : at + rows, :]


def causal(size, turned):
    row_id = lax.broadcasted_iota(jnp.int32, (size, size), 0)
    col_id = lax.broadcasted_iota(jnp.int32, (size, size), 1)
    return col_id >= row_id if turned else row_id >= col_id


def near_state(ctx_ref, refs, h, reverse):
    total = None
    for n, ref in enumerate(refs):
        value = ref[h].astype(F32)
        if n < QUAD - 1:
            low = jnp.bitwise_and(ctx_ref[0], 1 if n == 0 else 2) == 0
            value = jnp.where(low if reverse else jnp.logical_not(low), value, 0.0)
        total = value if total is None else total + value
    return total


def query_body(places, sub, parts, place_ref, ctx_ref, key_ref, value_ref, *refs):
    prev_refs, refs = refs[:parts], refs[parts:]
    grad_refs, (out_ref, done_ref, grad) = refs[: len(places)], refs[len(places) :]
    gather_grad(place_ref, grad_refs, places, sub, grad)
    keep = causal(sub, False)
    rows = [slice(at, at + sub) for at in range(0, key_ref.shape[0], sub)]
    for h in range(key_ref.shape[1] // HEAD_DIM):
        cols = head_cols(h)
        scores = [dot(grad[at, cols], value_ref[at, cols], NT) for at in rows]
        states = [near_state(ctx_ref, prev_refs, h, False)]
        for at in rows[:-1]:
            states.append(states[-1] + dot(key_ref[at, cols], value_ref[at, cols], TN))
        totals = [dot(grad[at, cols], state.astype(BF16), NT) for at, state in zip(rows, states)]
        scores = [jnp.where(keep, score, 0.0).astype(BF16) for score in scores]
        for at, score, total in zip(rows, scores, totals):
            total = total + dot(score, key_ref[at, cols], NN)
            out_ref[at, cols] = total
            done_ref[at, cols] = total.astype(BF16)


def later_body(sub, parts, place_ref, ctx_ref, query_ref, key_ref, value_ref, grad, *refs):
    near_ref, far_ref = refs[:2]
    next_refs, (key_out, value_out, key_done, value_done) = refs[2 : 2 + parts], refs[2 + parts :]
    place = place_ref[0]
    keep = causal(sub, True)
    rows = [slice(at, at + sub) for at in range(0, key_ref.shape[0], sub)]
    masked = lambda scores: [jnp.where(keep, score, 0.0).astype(BF16) for score in scores]
    for h in range(key_ref.shape[1] // HEAD_DIM):
        cols = head_cols(h)
        scores = [dot(value_ref[at, cols], grad[at, cols], NT) for at in rows]
        attn = [dot(key_ref[at, cols], query_ref[at, cols], NT) for at in rows]
        later = near_state(ctx_ref, next_refs, h, True)
        own = [near_ref[0, h], near_ref[1, h], far_ref[0, h], far_ref[1, h]]
        states = []
        for n in range(len(rows)):
            total = later
            for flip, state in enumerate(own):
                total = total + jnp.where(jnp.bitwise_xor(place, flip) > n, state, 0.0)
            states.append(total.astype(BF16))
        scores = masked(scores)
        for at, score, state in zip(rows, scores, states):
            total = dot(value_ref[at, cols], state, NT) + dot(score, query_ref[at, cols], NN)
            key_out[at, cols] = total
            key_done[at, cols] = total.astype(BF16)
        attn = masked(attn)
        for at, score, state in zip(rows, attn, states):
            total = dot(key_ref[at, cols], state, NN) + dot(score, grad[at, cols], NN)
            value_out[at, cols] = total
            value_done[at, cols] = total.astype(BF16)


def query_products(place, ctx, key_rows, value_rows, prevs, grads, places, sub):
    tokens, width = key_rows.shape
    return pl.pallas_call(
        functools.partial(query_body, places, sub, len(prevs)),
        out_shape=(
            jax.ShapeDtypeStruct((tokens, width), F32),
            jax.ShapeDtypeStruct((tokens, width), BF16),
            jax.ShapeDtypeStruct((tokens, width), BF16),
        ),
        in_specs=[smem(), smem()] + [vmem()] * (2 + len(prevs) + len(grads)),
        out_specs=(vmem(),) * 3,
        compiler_params=params(16),
        cost_estimate=cost(4 * tokens * tokens * width, 8 * tokens * width),
        name="query_products",
    )(place, ctx, key_rows, value_rows, *prevs, *grads)


def later_products(place, ctx, query_rows, key_rows, value_rows, grad_rows, near, far, nexts, sub):
    tokens, width = key_rows.shape
    return pl.pallas_call(
        functools.partial(later_body, sub, len(nexts)),
        out_shape=(jax.ShapeDtypeStruct((tokens, width), F32),) * 2
        + (jax.ShapeDtypeStruct((tokens, width), BF16),) * 2,
        in_specs=[smem(), smem()] + [vmem()] * (6 + len(nexts)),
        out_specs=(vmem(),) * 4,
        compiler_params=params(16),
        cost_estimate=cost(8 * tokens * tokens * width, 10 * tokens * width),
        name="later_products",
    )(place, ctx, query_rows, key_rows, value_rows, grad_rows, near, far, *nexts)


def end_body(sub, ctx_ref, half_ref, got_ref, key_ref, value_ref, grad_ref, *refs):
    part_refs, (out_refs, done, sems) = refs[:3], (refs[-5:-2], refs[-2], refs[-1])
    upper = ctx_ref[0] >= half_ref[0]
    lefts, dims = (grad_ref, value_ref, key_ref), (NT, NT, NN)

    def renew(which):
        copies = []
        for n in range(key_ref.shape[0] // sub):
            rows = slice(n * sub, (n + 1) * sub)
            for k in which:
                for h in range(got_ref.shape[0]):
                    cols = head_cols(h)
                    add = dot(lefts[k][rows, cols], got_ref[h], dims[k])
                    done[k, rows, cols] = (part_refs[k][rows, cols] + add).astype(BF16)
                copy = pltpu.make_async_copy(
                    done.at[k, pl.ds(n * sub, sub), :],
                    out_refs[k].at[pl.ds(n * sub, sub), :],
                    sems.at[k, n],
                )
                copy.start()
                copies.append(copy)
        for copy in copies:
            copy.wait()

    @pl.when(upper)
    def _():
        renew((0,))

    @pl.when(jnp.logical_not(upper))
    def _():
        renew((1, 2))


def end_products(ctx, half, got, key_rows, value_rows, grad_rows, parts, dones, sub):
    tokens, width = key_rows.shape
    return pl.pallas_call(
        functools.partial(end_body, sub),
        out_shape=(jax.ShapeDtypeStruct((tokens, width), BF16),) * 3,
        in_specs=[smem(), smem()] + [vmem()] * 7 + [hbm()] * 3,
        out_specs=(hbm(),) * 3,
        scratch_shapes=[
            pltpu.VMEM((3, tokens, width), BF16),
            pltpu.SemaphoreType.DMA((3, tokens // sub)),
        ],
        input_output_aliases={9 + k: k for k in range(3)},
        compiler_params=params(16),
        cost_estimate=cost(6 * tokens * width * HEAD_DIM, 16 * tokens * width),
        name="end_products",
    )(ctx, half, got, key_rows, value_rows, grad_rows, *parts, *dones)


def scan_states(wide, short, reverse, ties, name):
    size = lax.axis_size("ctx")
    send = lambda payload, pairs: lax.ppermute(payload, "ctx", pairs)
    received = [send(short, [(i, i ^ k) for i in range(size)]) for k in range(1, QUAD)]
    reach = QUAD
    while reach < size // 2:
        payload = group_state(wide, received, ties if reach == QUAD else [], "%s_%d" % (name, reach))
        if reverse:
            pairs = [(i + reach, i) for i in range(size - reach)]
        else:
            pairs = [(i, i + reach) for i in range(size - reach)]
        received.append(send(payload, pairs))
        reach *= 2
    return received


def per_device(out_grad, keep_mask, out_weight, query_rows, key_rows, value_rows):
    size = lax.axis_size("head")
    place = lax.axis_index("head").astype(jnp.int32).reshape(1)
    ctx = lax.axis_index("ctx").astype(jnp.int32).reshape(1)
    own_rows = out_grad.shape[0]
    half = jnp.full((1,), lax.axis_size("ctx") // 2, jnp.int32)
    unit = own_rows // 16
    split = 9 * unit

    def swap(array, distance):
        return lax.ppermute(array, "head", [(i, i ^ distance) for i in range(size)])

    first, *near_first = mask_rows(out_grad, keep_mask, 0, (5 * unit, 4 * unit), "mask_first")
    last, *near_last = mask_rows(out_grad, keep_mask, split, (4 * unit, 3 * unit), "mask_last")
    far_first, far_last = swap(first, 2), swap(last, 2)
    kv_wide, kv_short = kv_state(key_rows, value_rows)
    prevs = scan_states(kv_wide, kv_short, False, [], "prev")
    near = [swap(piece, 1) for piece in near_first + near_last]

    part = functools.partial(grad_part, place, query_rows, out_weight, own_rows)
    grads, places, states = [], [], []

    def run(befores, pieces, arrays, name, mib=20):
        got = part(befores, pieces, arrays, name, mib)
        at, spots = 0, []
        for (flip, row), array in zip(pieces, arrays):
            spots.append((at, array.shape[0], flip, row))
            at += array.shape[0]
        grads.append(got[0])
        places.append(tuple(spots))
        states.append(got[1])
        return got

    pieces = ((0, 0), (0, split), (1, 0), (1, 5 * unit), (1, split), (1, split + 4 * unit))
    run([], pieces, [first, last] + near, "grad_near", 60)

    prev_sum = group_state(kv_wide, prevs, [states[0]], "prev_sum")

    far_first = after(far_first, prev_sum, states[0])
    run([], ((2, 0), (3, 0)), [far_first, swap(far_first, 1)], "grad_far")
    _, far, wide, short = run(
        [states[1], states[0]],
        ((2, split), (3, split)),
        [far_last, swap(far_last, 1)],
        "grad_last",
    )

    spots = tuple(places)
    query_part, query_done, grad_rows = query_products(place, ctx, key_rows, value_rows, prevs, grads, spots, own_rows)
    nexts = scan_states(wide, short, True, [query_part], "next")
    nexts[-1] = after(nexts[-1], query_part)
    payload = swap_state(ctx, half, prev_sum, wide, nexts)
    size = lax.axis_size("ctx")
    got = lax.ppermute(payload, "ctx", [(i, (i + size // 2) % size) for i in range(size)])
    key_part, value_part, key_done, value_done = later_products(
        place, ctx, query_rows, key_rows, value_rows, grad_rows, states[0], far, nexts, own_rows
    )
    parts = (query_part, key_part, value_part)
    dones = (query_done, key_done, value_done)
    return end_products(ctx, half, got, key_rows, value_rows, grad_rows, parts, dones, own_rows)


def solution(mesh):
    placed = (
        P(("ctx", "head"), None),
        P(("ctx", "head"), None),
        P("head", None),
        P("ctx", "head"),
        P("ctx", "head"),
        P("ctx", "head"),
    )
    return jax.shard_map(
        per_device,
        mesh=mesh,
        in_specs=placed,
        out_specs=(P("ctx", "head"), P("ctx", "head"), P("ctx", "head")),
        check_vma=False,
    )
```

```python
import functools

import jax
import jax.numpy as jnp
from jax import lax
from jax.experimental import pallas as pl
from jax.experimental.pallas import tpu as pltpu
from jax.sharding import PartitionSpec as P

HEAD_DIM = 128
QUAD = 4
KEEP_SCALE = 1.0 / 0.9
F32 = jnp.float32
BF16 = jnp.bfloat16
NT = (((1,), (1,)), ((), ()))
NN = (((1,), (0,)), ((), ()))
TN = (((0,), (0,)), ((), ()))
MIB = 1024 * 1024


def dot(left, right, dims):
    return lax.dot_general(left, right, dims, preferred_element_type=F32)


def vmem():
    return pl.BlockSpec(memory_space=pltpu.VMEM)


def smem():
    return pl.BlockSpec(memory_space=pltpu.SMEM)


def hbm():
    return pl.BlockSpec(memory_space=pltpu.HBM)


def params(mib):
    return pltpu.CompilerParams(vmem_limit_bytes=mib * MIB)


def cost(flops, nbytes):
    return pl.CostEstimate(flops=flops, bytes_accessed=nbytes, transcendentals=0)


def head_cols(h):
    return slice(h * HEAD_DIM, (h + 1) * HEAD_DIM)


def masked_rows(grad, keep):
    return (grad.astype(F32) * keep.astype(F32) * KEEP_SCALE).astype(BF16)


def fetch(source, target, sems, row, rows, pieces):
    size = rows // pieces
    copies = []
    for n in range(pieces):
        copy = pltpu.make_async_copy(
            source.at[pl.ds(row + n * size, size), :],
            target.at[pl.ds(n * size, size), :],
            sems.at[n],
        )
        copy.start()
        copies.append(copy)
    return copies


def mask_body(row, grad_ref, keep_ref, *refs):
    out_refs, (grad, keep, masked, grad_sems, keep_sems, out_sems) = refs[:-6], refs[-6:]
    rows = grad.shape[0]
    pieces = keep_sems.shape[0]
    size = rows // pieces
    keep_copies = fetch(keep_ref, keep, keep_sems, row, rows, pieces)
    grad_copies = fetch(grad_ref, grad, grad_sems, row, rows, pieces)
    copies = []

    def send(at, count, target):
        copy = pltpu.make_async_copy(masked.at[pl.ds(at, count), :], target, out_sems.at[len(copies)])
        copy.start()
        copies.append(copy)

    waiting, at = [], 0
    for ref in out_refs[1:]:
        waiting.append((at, ref))
        at += ref.shape[0]
    for n in range(pieces):
        keep_copies[n].wait()
        grad_copies[n].wait()
        low, high = n * size, (n + 1) * size
        masked[low:high, :] = masked_rows(grad[low:high, :], keep[low:high, :])
        send(low, size, out_refs[0].at[pl.ds(low, size), :])
        while waiting and waiting[0][0] + waiting[0][1].shape[0] <= high:
            at, ref = waiting.pop(0)
            send(at, ref.shape[0], ref)
    for copy in copies:
        copy.wait()


def mask_rows(out_grad, keep_mask, row, split, name):
    model = out_grad.shape[1]
    rows = sum(split)
    pieces = rows // 16 if rows % 48 else rows // 48
    return pl.pallas_call(
        functools.partial(mask_body, row),
        out_shape=tuple(jax.ShapeDtypeStruct((n, model), BF16) for n in [rows] + list(split)),
        in_specs=[hbm(), hbm()],
        out_specs=(hbm(),) * (1 + len(split)),
        scratch_shapes=[
            pltpu.VMEM((rows, model), BF16),
            pltpu.VMEM((rows, model), jnp.int32),
            pltpu.VMEM((rows, model), BF16),
            pltpu.SemaphoreType.DMA((pieces,)),
            pltpu.SemaphoreType.DMA((pieces,)),
            pltpu.SemaphoreType.DMA((pieces + len(split),)),
        ],
        compiler_params=params(56),
        cost_estimate=cost(1, 1),
        name=name,
    )(out_grad, keep_mask)


def kv_body(key_ref, value_ref, wide_ref, short_ref):
    for h in range(wide_ref.shape[0]):
        total = dot(key_ref[:, head_cols(h)], value_ref[:, head_cols(h)], TN)
        wide_ref[h] = total
        short_ref[h] = total.astype(BF16)


def kv_state(key_rows, value_rows):
    heads = key_rows.shape[1] // HEAD_DIM
    shape = (heads, HEAD_DIM, HEAD_DIM)
    return pl.pallas_call(
        kv_body,
        out_shape=(jax.ShapeDtypeStruct(shape, F32), jax.ShapeDtypeStruct(shape, BF16)),
        in_specs=[vmem(), vmem()],
        out_specs=(vmem(), vmem()),
        compiler_params=params(12),
        cost_estimate=cost(1, 1),
        name="kv_state",
    )(key_rows, value_rows)


def group_body(count, wide_ref, *refs):
    total = wide_ref[...]
    for ref in refs[:count]:
        total = total + ref[...].astype(F32)
    refs[-1][...] = total.astype(BF16)


def after(array, *others):
    return lax.optimization_barrier((array,) + others)[0]


def group_state(wide, received, ties, name):
    received = received[:-1] + [after(received[-1], *ties)]
    return pl.pallas_call(
        functools.partial(group_body, len(received)),
        out_shape=jax.ShapeDtypeStruct(wide.shape, BF16),
        in_specs=[vmem()] * (1 + len(received)),
        out_specs=vmem(),
        compiler_params=params(4),
        cost_estimate=cost(1, 1),
        name=name,
    )(wide, *received)


def swap_body(count, ctx_ref, half_ref, prev_ref, wide_ref, *refs):
    total = wide_ref[...]
    for ref in refs[:count]:
        total = total + ref[...].astype(F32)
    upper = ctx_ref[0] >= half_ref[0]
    refs[-1][...] = jnp.where(upper, total, prev_ref[...].astype(F32)).astype(BF16)


def swap_state(ctx, half, prev, wide, received):
    return pl.pallas_call(
        functools.partial(swap_body, len(received)),
        out_shape=jax.ShapeDtypeStruct(wide.shape, BF16),
        in_specs=[smem(), smem()] + [vmem()] * (2 + len(received)),
        out_specs=vmem(),
        compiler_params=params(4),
        cost_estimate=cost(1, 1),
        name="swap_state",
    )(ctx, half, prev, wide, *received)


def grad_body(pieces, sub, befores, last, *refs):
    place_ref, query_ref, weight_ref = refs[:3]
    refs = refs[3:]
    before_refs, refs = refs[:befores], refs[befores:]
    masked_refs, refs = refs[: len(pieces)], refs[len(pieces) :]
    grad_ref, state_ref = refs[:2]
    masked, query, sems = refs[-3:]
    copies = []
    place = place_ref[0]
    spots, at = [], 0
    for ref, (flip, row) in zip(masked_refs, pieces):
        rows = ref.shape[0]
        copy = pltpu.make_async_copy(ref, masked.at[pl.ds(at, rows), :], sems.at[len(copies)])
        copy.start()
        copies.append(copy)
        start = pl.multiple_of(jnp.bitwise_xor(place, flip) * sub + row, 16)
        query[at : at + rows, :] = query_ref[pl.ds(start, rows), :]
        if spots and spots[-1][0] == flip:
            spots[-1][2] = at + rows
        else:
            spots.append([flip, at, at + rows])
        at += rows
    spots = [slice(low, high) for _, low, high in spots]
    for copy in copies:
        copy.wait()
    grad = dot(masked[...], weight_ref[...], NT).astype(BF16)
    grad_ref[...] = grad
    for h in range(state_ref.shape[1]):
        total = None
        for n, rows in enumerate(spots):
            state = dot(query[rows, head_cols(h)], grad[rows, head_cols(h)], TN)
            if last:
                state = state + before_refs[0][n, h]
                other = before_refs[1][n, h]
                total = state + other if total is None else total + (state + other)
            state_ref[n, h] = state
        if last:
            wide_ref, short_ref = refs[2:4]
            wide_ref[h] = total
            short_ref[h] = total.astype(BF16)


def grad_part(place, query_rows, out_weight, sub, befores, pieces, arrays, name, mib=20):
    width, model = out_weight.shape
    heads = width // HEAD_DIM
    rows = sum(a.shape[0] for a in arrays)
    shape = (heads, HEAD_DIM, HEAD_DIM)
    last = len(befores) > 0
    out_shape = [
        jax.ShapeDtypeStruct((rows, width), BF16),
        jax.ShapeDtypeStruct((2,) + shape, F32),
    ]
    if last:
        out_shape += [jax.ShapeDtypeStruct(shape, F32), jax.ShapeDtypeStruct(shape, BF16)]
    operands = [place, query_rows, out_weight] + list(befores) + list(arrays)
    return pl.pallas_call(
        functools.partial(grad_body, pieces, sub, len(befores), last),
        out_shape=tuple(out_shape),
        in_specs=[smem()] + [vmem()] * (2 + len(befores)) + [hbm()] * len(arrays),
        out_specs=tuple(vmem() for _ in out_shape),
        scratch_shapes=[
            pltpu.VMEM((rows, model), BF16),
            pltpu.VMEM((rows, width), BF16),
            pltpu.SemaphoreType.DMA((len(arrays),)),
        ],
        compiler_params=params(mib),
        cost_estimate=cost(1, 1),
        name=name,
    )(*operands)


def gather_grad(place_ref, grad_refs, places, own_rows, grad):
    place = place_ref[0]
    for ref, pieces in zip(grad_refs, places):
        for at, rows, flip, row in pieces:
            start = pl.multiple_of(jnp.bitwise_xor(place, flip) * own_rows + row, 16)
            grad[pl.ds(start, rows), :] = ref[at : at + rows, :]


def causal(size, turned):
    row_id = lax.broadcasted_iota(jnp.int32, (size, size), 0)
    col_id = lax.broadcasted_iota(jnp.int32, (size, size), 1)
    return col_id >= row_id if turned else row_id >= col_id


def near_state(ctx_ref, refs, h, reverse):
    total = None
    for n, ref in enumerate(refs):
        value = ref[h].astype(F32)
        if n < QUAD - 1:
            low = jnp.bitwise_and(ctx_ref[0], 1 if n == 0 else 2) == 0
            value = jnp.where(low if reverse else jnp.logical_not(low), value, 0.0)
        total = value if total is None else total + value
    return total


def query_body(places, sub, parts, place_ref, ctx_ref, key_ref, value_ref, *refs):
    prev_refs, refs = refs[:parts], refs[parts:]
    grad_refs, (out_ref, done_ref, grad) = refs[: len(places)], refs[len(places) :]
    gather_grad(place_ref, grad_refs, places, sub, grad)
    keep = causal(sub, False)
    rows = [slice(at, at + sub) for at in range(0, key_ref.shape[0], sub)]
    for h in range(key_ref.shape[1] // HEAD_DIM):
        cols = head_cols(h)
        scores = [dot(grad[at, cols], value_ref[at, cols], NT) for at in rows]
        states = [near_state(ctx_ref, prev_refs, h, False)]
        for at in rows[:-1]:
            states.append(states[-1] + dot(key_ref[at, cols], value_ref[at, cols], TN))
        totals = [dot(grad[at, cols], state.astype(BF16), NT) for at, state in zip(rows, states)]
        scores = [jnp.where(keep, score, 0.0).astype(BF16) for score in scores]
        for at, score, total in zip(rows, scores, totals):
            total = total + dot(score, key_ref[at, cols], NN)
            out_ref[at, cols] = total
            done_ref[at, cols] = total.astype(BF16)


def later_body(sub, parts, place_ref, ctx_ref, query_ref, key_ref, value_ref, grad, *refs):
    near_ref, far_ref = refs[:2]
    next_refs, (key_out, value_out, key_done, value_done) = refs[2 : 2 + parts], refs[2 + parts :]
    place = place_ref[0]
    keep = causal(sub, True)
    rows = [slice(at, at + sub) for at in range(0, key_ref.shape[0], sub)]
    masked = lambda scores: [jnp.where(keep, score, 0.0).astype(BF16) for score in scores]
    for h in range(key_ref.shape[1] // HEAD_DIM):
        cols = head_cols(h)
        scores = [dot(value_ref[at, cols], grad[at, cols], NT) for at in rows]
        attn = [dot(key_ref[at, cols], query_ref[at, cols], NT) for at in rows]
        later = near_state(ctx_ref, next_refs, h, True)
        own = [near_ref[0, h], near_ref[1, h], far_ref[0, h], far_ref[1, h]]
        states = []
        for n in range(len(rows)):
            total = later
            for flip, state in enumerate(own):
                total = total + jnp.where(jnp.bitwise_xor(place, flip) > n, state, 0.0)
            states.append(total.astype(BF16))
        scores = masked(scores)
        for at, score, state in zip(rows, scores, states):
            total = dot(value_ref[at, cols], state, NT) + dot(score, query_ref[at, cols], NN)
            key_out[at, cols] = total
            key_done[at, cols] = total.astype(BF16)
        attn = masked(attn)
        for at, score, state in zip(rows, attn, states):
            total = dot(key_ref[at, cols], state, NN) + dot(score, grad[at, cols], NN)
            value_out[at, cols] = total
            value_done[at, cols] = total.astype(BF16)


def query_products(place, ctx, key_rows, value_rows, prevs, grads, places, sub):
    tokens, width = key_rows.shape
    return pl.pallas_call(
        functools.partial(query_body, places, sub, len(prevs)),
        out_shape=(
            jax.ShapeDtypeStruct((tokens, width), F32),
            jax.ShapeDtypeStruct((tokens, width), BF16),
            jax.ShapeDtypeStruct((tokens, width), BF16),
        ),
        in_specs=[smem(), smem()] + [vmem()] * (2 + len(prevs) + len(grads)),
        out_specs=(vmem(),) * 3,
        compiler_params=params(16),
        cost_estimate=cost(4 * tokens * tokens * width, 8 * tokens * width),
        name="query_products",
    )(place, ctx, key_rows, value_rows, *prevs, *grads)


def later_products(place, ctx, query_rows, key_rows, value_rows, grad_rows, near, far, nexts, sub):
    tokens, width = key_rows.shape
    return pl.pallas_call(
        functools.partial(later_body, sub, len(nexts)),
        out_shape=(jax.ShapeDtypeStruct((tokens, width), F32),) * 2
        + (jax.ShapeDtypeStruct((tokens, width), BF16),) * 2,
        in_specs=[smem(), smem()] + [vmem()] * (6 + len(nexts)),
        out_specs=(vmem(),) * 4,
        compiler_params=params(16),
        cost_estimate=cost(8 * tokens * tokens * width, 10 * tokens * width),
        name="later_products",
    )(place, ctx, query_rows, key_rows, value_rows, grad_rows, near, far, *nexts)


def end_body(sub, ctx_ref, half_ref, got_ref, key_ref, value_ref, grad_ref, *refs):
    part_refs, (out_refs, done, sems) = refs[:3], (refs[-5:-2], refs[-2], refs[-1])
    upper = ctx_ref[0] >= half_ref[0]
    lefts, dims = (grad_ref, value_ref, key_ref), (NT, NT, NN)

    def renew(which):
        copies = []
        for n in range(key_ref.shape[0] // sub):
            rows = slice(n * sub, (n + 1) * sub)
            for k in which:
                for h in range(got_ref.shape[0]):
                    cols = head_cols(h)
                    add = dot(lefts[k][rows, cols], got_ref[h], dims[k])
                    done[k, rows, cols] = (part_refs[k][rows, cols] + add).astype(BF16)
                copy = pltpu.make_async_copy(
                    done.at[k, pl.ds(n * sub, sub), :],
                    out_refs[k].at[pl.ds(n * sub, sub), :],
                    sems.at[k, n],
                )
                copy.start()
                copies.append(copy)
        for copy in copies:
            copy.wait()

    @pl.when(upper)
    def _():
        renew((0,))

    @pl.when(jnp.logical_not(upper))
    def _():
        renew((1, 2))


def end_products(ctx, half, got, key_rows, value_rows, grad_rows, parts, dones, sub):
    tokens, width = key_rows.shape
    return pl.pallas_call(
        functools.partial(end_body, sub),
        out_shape=(jax.ShapeDtypeStruct((tokens, width), BF16),) * 3,
        in_specs=[smem(), smem()] + [vmem()] * 7 + [hbm()] * 3,
        out_specs=(hbm(),) * 3,
        scratch_shapes=[
            pltpu.VMEM((3, tokens, width), BF16),
            pltpu.SemaphoreType.DMA((3, tokens // sub)),
        ],
        input_output_aliases={9 + k: k for k in range(3)},
        compiler_params=params(16),
        cost_estimate=cost(6 * tokens * width * HEAD_DIM, 16 * tokens * width),
        name="end_products",
    )(ctx, half, got, key_rows, value_rows, grad_rows, *parts, *dones)


def scan_states(wide, short, reverse, ties, name):
    size = lax.axis_size("ctx")
    send = lambda payload, pairs: lax.ppermute(payload, "ctx", pairs)
    received = [send(short, [(i, i ^ k) for i in range(size)]) for k in range(1, QUAD)]
    reach = QUAD
    while reach < size // 2:
        payload = group_state(wide, received, ties if reach == QUAD else [], "%s_%d" % (name, reach))
        if reverse:
            pairs = [(i + reach, i) for i in range(size - reach)]
        else:
            pairs = [(i, i + reach) for i in range(size - reach)]
        received.append(send(payload, pairs))
        reach *= 2
    return received


def per_device(out_grad, keep_mask, out_weight, query_rows, key_rows, value_rows):
    size = lax.axis_size("head")
    place = lax.axis_index("head").astype(jnp.int32).reshape(1)
    ctx = lax.axis_index("ctx").astype(jnp.int32).reshape(1)
    own_rows = out_grad.shape[0]
    half = jnp.full((1,), lax.axis_size("ctx") // 2, jnp.int32)
    unit = own_rows // 16
    split = 9 * unit

    def swap(array, distance):
        return lax.ppermute(array, "head", [(i, i ^ distance) for i in range(size)])

    first, *near_first = mask_rows(out_grad, keep_mask, 0, (5 * unit, 4 * unit), "mask_first")
    last, *near_last = mask_rows(out_grad, keep_mask, split, (4 * unit, 3 * unit), "mask_last")
    far_first, far_last = swap(first, 2), swap(last, 2)
    kv_wide, kv_short = kv_state(key_rows, value_rows)
    prevs = scan_states(kv_wide, kv_short, False, [], "prev")
    near = [swap(piece, 1) for piece in near_first + near_last]

    part = functools.partial(grad_part, place, query_rows, out_weight, own_rows)
    grads, places, states = [], [], []

    def run(befores, pieces, arrays, name, mib=20):
        got = part(befores, pieces, arrays, name, mib)
        at, spots = 0, []
        for (flip, row), array in zip(pieces, arrays):
            spots.append((at, array.shape[0], flip, row))
            at += array.shape[0]
        grads.append(got[0])
        places.append(tuple(spots))
        states.append(got[1])
        return got

    pieces = ((0, 0), (0, split), (1, 0), (1, 5 * unit), (1, split), (1, split + 4 * unit))
    run([], pieces, [first, last] + near, "grad_near", 60)

    prev_sum = group_state(kv_wide, prevs, [states[0]], "prev_sum")

    far_first = after(far_first, prev_sum, states[0])
    run([], ((2, 0), (3, 0)), [far_first, swap(far_first, 1)], "grad_far")
    _, far, wide, short = run(
        [states[1], states[0]],
        ((2, split), (3, split)),
        [far_last, swap(far_last, 1)],
        "grad_last",
    )

    spots = tuple(places)
    query_part, query_done, grad_rows = query_products(place, ctx, key_rows, value_rows, prevs, grads, spots, own_rows)
    nexts = scan_states(wide, short, True, [query_part], "next")
    nexts[-1] = after(nexts[-1], query_part)
    payload = swap_state(ctx, half, prev_sum, wide, nexts)
    size = lax.axis_size("ctx")
    got = lax.ppermute(payload, "ctx", [(i, (i + size // 2) % size) for i in range(size)])
    key_part, value_part, key_done, value_done = later_products(
        place, ctx, query_rows, key_rows, value_rows, grad_rows, states[0], far, nexts, own_rows
    )
    parts = (query_part, key_part, value_part)
    dones = (query_done, key_done, value_done)
    return end_products(ctx, half, got, key_rows, value_rows, grad_rows, parts, dones, own_rows)


def solution(mesh):
    placed = (
        P(("ctx", "head"), None),
        P(("ctx", "head"), None),
        P("head", None),
        P("ctx", "head"),
        P("ctx", "head"),
        P("ctx", "head"),
    )
    return jax.shard_map(
        per_device,
        mesh=mesh,
        in_specs=placed,
        out_specs=(P("ctx", "head"), P("ctx", "head"), P("ctx", "head")),
        check_vma=False,
    )
```

```python
import functools

import jax
import jax.numpy as jnp
from jax import lax
from jax.experimental import pallas as pl
from jax.experimental.pallas import tpu as pltpu
from jax.sharding import PartitionSpec as P

HEAD_DIM = 128
QUAD = 4
KEEP_SCALE = 1.0 / 0.9
F32 = jnp.float32
BF16 = jnp.bfloat16
NT = (((1,), (1,)), ((), ()))
NN = (((1,), (0,)), ((), ()))
TN = (((0,), (0,)), ((), ()))
MIB = 1024 * 1024


def dot(left, right, dims):
    return lax.dot_general(left, right, dims, preferred_element_type=F32)


def vmem():
    return pl.BlockSpec(memory_space=pltpu.VMEM)


def smem():
    return pl.BlockSpec(memory_space=pltpu.SMEM)


def hbm():
    return pl.BlockSpec(memory_space=pltpu.HBM)


def params(mib):
    return pltpu.CompilerParams(vmem_limit_bytes=mib * MIB)


def cost(flops, nbytes):
    return pl.CostEstimate(flops=flops, bytes_accessed=nbytes, transcendentals=0)


def head_cols(h):
    return slice(h * HEAD_DIM, (h + 1) * HEAD_DIM)


def masked_rows(grad, keep):
    return (grad.astype(F32) * keep.astype(F32) * KEEP_SCALE).astype(BF16)


def fetch(source, target, sems, row, rows, pieces):
    size = rows // pieces
    copies = []
    for n in range(pieces):
        copy = pltpu.make_async_copy(
            source.at[pl.ds(row + n * size, size), :],
            target.at[pl.ds(n * size, size), :],
            sems.at[n],
        )
        copy.start()
        copies.append(copy)
    return copies


def mask_body(row, grad_ref, keep_ref, *refs):
    out_refs, (grad, keep, grad_sems, keep_sems) = refs[:-4], refs[-4:]
    rows = grad.shape[0]
    pieces = keep_sems.shape[0]
    size = rows // pieces
    keep_copies = fetch(keep_ref, keep, keep_sems, row, rows, pieces)
    grad_copies = fetch(grad_ref, grad, grad_sems, row, rows, pieces)
    for n in range(pieces):
        keep_copies[n].wait()
        grad_copies[n].wait()
        low, high = n * size, (n + 1) * size
        value = masked_rows(grad[low:high, :], keep[low:high, :])
        out_refs[0][low:high, :] = value
        at = 0
        for ref in out_refs[1:]:
            end = at + ref.shape[0]
            top, bottom = max(low, at), min(high, end)
            if top < bottom:
                ref[top - at : bottom - at, :] = value[top - low : bottom - low, :]
            at = end


def mask_rows(out_grad, keep_mask, row, split, name):
    model = out_grad.shape[1]
    rows = sum(split)
    pieces = rows // 16 if rows % 48 else rows // 48
    return pl.pallas_call(
        functools.partial(mask_body, row),
        out_shape=tuple(jax.ShapeDtypeStruct((n, model), BF16) for n in [rows] + list(split)),
        in_specs=[hbm(), hbm()],
        out_specs=(vmem(),) * (1 + len(split)),
        scratch_shapes=[
            pltpu.VMEM((rows, model), BF16),
            pltpu.VMEM((rows, model), jnp.int32),
            pltpu.SemaphoreType.DMA((pieces,)),
            pltpu.SemaphoreType.DMA((pieces,)),
        ],
        compiler_params=params(56),
        cost_estimate=cost(1, 1),
        name=name,
    )(out_grad, keep_mask)


def kv_body(key_ref, value_ref, wide_ref, short_ref):
    for h in range(wide_ref.shape[0]):
        total = dot(key_ref[:, head_cols(h)], value_ref[:, head_cols(h)], TN)
        wide_ref[h] = total
        short_ref[h] = total.astype(BF16)


def kv_state(key_rows, value_rows):
    heads = key_rows.shape[1] // HEAD_DIM
    shape = (heads, HEAD_DIM, HEAD_DIM)
    return pl.pallas_call(
        kv_body,
        out_shape=(jax.ShapeDtypeStruct(shape, F32), jax.ShapeDtypeStruct(shape, BF16)),
        in_specs=[vmem(), vmem()],
        out_specs=(vmem(), vmem()),
        compiler_params=params(12),
        cost_estimate=cost(1, 1),
        name="kv_state",
    )(key_rows, value_rows)


def group_body(count, wide_ref, *refs):
    total = wide_ref[...]
    for ref in refs[:count]:
        total = total + ref[...].astype(F32)
    refs[-1][...] = total.astype(BF16)


def after(array, *others):
    return lax.optimization_barrier((array,) + others)[0]


def group_state(wide, received, ties, name):
    received = received[:-1] + [after(received[-1], *ties)]
    return pl.pallas_call(
        functools.partial(group_body, len(received)),
        out_shape=jax.ShapeDtypeStruct(wide.shape, BF16),
        in_specs=[vmem()] * (1 + len(received)),
        out_specs=vmem(),
        compiler_params=params(4),
        cost_estimate=cost(1, 1),
        name=name,
    )(wide, *received)


def swap_body(count, ctx_ref, half_ref, prev_ref, wide_ref, *refs):
    total = wide_ref[...]
    for ref in refs[:count]:
        total = total + ref[...].astype(F32)
    upper = ctx_ref[0] >= half_ref[0]
    refs[-1][...] = jnp.where(upper, total, prev_ref[...].astype(F32)).astype(BF16)


def swap_state(ctx, half, prev, wide, received):
    return pl.pallas_call(
        functools.partial(swap_body, len(received)),
        out_shape=jax.ShapeDtypeStruct(wide.shape, BF16),
        in_specs=[smem(), smem()] + [vmem()] * (2 + len(received)),
        out_specs=vmem(),
        compiler_params=params(4),
        cost_estimate=cost(1, 1),
        name="swap_state",
    )(ctx, half, prev, wide, *received)


def grad_body(pieces, sub, befores, last, *refs):
    place_ref, query_ref, weight_ref = refs[:3]
    refs = refs[3:]
    before_refs, refs = refs[:befores], refs[befores:]
    masked_refs, refs = refs[: len(pieces)], refs[len(pieces) :]
    grad_ref, state_ref = refs[:2]
    masked, query, sems = refs[-3:]
    copies = []
    place = place_ref[0]
    spots, at = [], 0
    for ref, (flip, row) in zip(masked_refs, pieces):
        rows = ref.shape[0]
        copy = pltpu.make_async_copy(ref, masked.at[pl.ds(at, rows), :], sems.at[len(copies)])
        copy.start()
        copies.append(copy)
        start = pl.multiple_of(jnp.bitwise_xor(place, flip) * sub + row, 16)
        query[at : at + rows, :] = query_ref[pl.ds(start, rows), :]
        if spots and spots[-1][0] == flip:
            spots[-1][2] = at + rows
        else:
            spots.append([flip, at, at + rows])
        at += rows
    spots = [slice(low, high) for _, low, high in spots]
    for copy in copies:
        copy.wait()
    grad = dot(masked[...], weight_ref[...], NT).astype(BF16)
    grad_ref[...] = grad
    for h in range(state_ref.shape[1]):
        total = None
        for n, rows in enumerate(spots):
            state = dot(query[rows, head_cols(h)], grad[rows, head_cols(h)], TN)
            if last:
                state = state + before_refs[0][n, h]
                other = before_refs[1][n, h]
                total = state + other if total is None else total + (state + other)
            state_ref[n, h] = state
        if last:
            wide_ref, short_ref = refs[2:4]
            wide_ref[h] = total
            short_ref[h] = total.astype(BF16)


def grad_part(place, query_rows, out_weight, sub, befores, pieces, arrays, name, mib=20):
    width, model = out_weight.shape
    heads = width // HEAD_DIM
    rows = sum(a.shape[0] for a in arrays)
    shape = (heads, HEAD_DIM, HEAD_DIM)
    last = len(befores) > 0
    out_shape = [
        jax.ShapeDtypeStruct((rows, width), BF16),
        jax.ShapeDtypeStruct((2,) + shape, F32),
    ]
    if last:
        out_shape += [jax.ShapeDtypeStruct(shape, F32), jax.ShapeDtypeStruct(shape, BF16)]
    operands = [place, query_rows, out_weight] + list(befores) + list(arrays)
    return pl.pallas_call(
        functools.partial(grad_body, pieces, sub, len(befores), last),
        out_shape=tuple(out_shape),
        in_specs=[smem()] + [vmem()] * (2 + len(befores)) + [hbm()] * len(arrays),
        out_specs=tuple(vmem() for _ in out_shape),
        scratch_shapes=[
            pltpu.VMEM((rows, model), BF16),
            pltpu.VMEM((rows, width), BF16),
            pltpu.SemaphoreType.DMA((len(arrays),)),
        ],
        compiler_params=params(mib),
        cost_estimate=cost(1, 1),
        name=name,
    )(*operands)


def gather_grad(place_ref, grad_refs, places, own_rows, grad):
    place = place_ref[0]
    for ref, pieces in zip(grad_refs, places):
        for at, rows, flip, row in pieces:
            start = pl.multiple_of(jnp.bitwise_xor(place, flip) * own_rows + row, 16)
            grad[pl.ds(start, rows), :] = ref[at : at + rows, :]


def causal(size, turned):
    row_id = lax.broadcasted_iota(jnp.int32, (size, size), 0)
    col_id = lax.broadcasted_iota(jnp.int32, (size, size), 1)
    return col_id >= row_id if turned else row_id >= col_id


def near_state(ctx_ref, refs, h, reverse):
    total = None
    for n, ref in enumerate(refs):
        value = ref[h].astype(F32)
        if n < QUAD - 1:
            low = jnp.bitwise_and(ctx_ref[0], 1 if n == 0 else 2) == 0
            value = jnp.where(low if reverse else jnp.logical_not(low), value, 0.0)
        total = value if total is None else total + value
    return total


def query_body(places, sub, parts, place_ref, ctx_ref, key_ref, value_ref, *refs):
    prev_refs, refs = refs[:parts], refs[parts:]
    grad_refs, (out_ref, done_ref, grad) = refs[: len(places)], refs[len(places) :]
    gather_grad(place_ref, grad_refs, places, sub, grad)
    keep = causal(sub, False)
    rows = [slice(at, at + sub) for at in range(0, key_ref.shape[0], sub)]
    for h in range(key_ref.shape[1] // HEAD_DIM):
        cols = head_cols(h)
        scores = [dot(grad[at, cols], value_ref[at, cols], NT) for at in rows]
        states = [near_state(ctx_ref, prev_refs, h, False)]
        for at in rows[:-1]:
            states.append(states[-1] + dot(key_ref[at, cols], value_ref[at, cols], TN))
        totals = [dot(grad[at, cols], state.astype(BF16), NT) for at, state in zip(rows, states)]
        scores = [jnp.where(keep, score, 0.0).astype(BF16) for score in scores]
        for at, score, total in zip(rows, scores, totals):
            total = total + dot(score, key_ref[at, cols], NN)
            out_ref[at, cols] = total
            done_ref[at, cols] = total.astype(BF16)


def later_body(sub, parts, place_ref, ctx_ref, query_ref, key_ref, value_ref, grad, *refs):
    near_ref, far_ref = refs[:2]
    next_refs, (key_out, value_out, key_done, value_done) = refs[2 : 2 + parts], refs[2 + parts :]
    place = place_ref[0]
    keep = causal(sub, True)
    rows = [slice(at, at + sub) for at in range(0, key_ref.shape[0], sub)]
    masked = lambda scores: [jnp.where(keep, score, 0.0).astype(BF16) for score in scores]
    for h in range(key_ref.shape[1] // HEAD_DIM):
        cols = head_cols(h)
        scores = [dot(value_ref[at, cols], grad[at, cols], NT) for at in rows]
        attn = [dot(key_ref[at, cols], query_ref[at, cols], NT) for at in rows]
        later = near_state(ctx_ref, next_refs, h, True)
        own = [near_ref[0, h], near_ref[1, h], far_ref[0, h], far_ref[1, h]]
        states = []
        for n in range(len(rows)):
            total = later
            for flip, state in enumerate(own):
                total = total + jnp.where(jnp.bitwise_xor(place, flip) > n, state, 0.0)
            states.append(total.astype(BF16))
        scores = masked(scores)
        for at, score, state in zip(rows, scores, states):
            total = dot(value_ref[at, cols], state, NT) + dot(score, query_ref[at, cols], NN)
            key_out[at, cols] = total
            key_done[at, cols] = total.astype(BF16)
        attn = masked(attn)
        for at, score, state in zip(rows, attn, states):
            total = dot(key_ref[at, cols], state, NN) + dot(score, grad[at, cols], NN)
            value_out[at, cols] = total
            value_done[at, cols] = total.astype(BF16)


def query_products(place, ctx, key_rows, value_rows, prevs, grads, places, sub):
    tokens, width = key_rows.shape
    return pl.pallas_call(
        functools.partial(query_body, places, sub, len(prevs)),
        out_shape=(
            jax.ShapeDtypeStruct((tokens, width), F32),
            jax.ShapeDtypeStruct((tokens, width), BF16),
            jax.ShapeDtypeStruct((tokens, width), BF16),
        ),
        in_specs=[smem(), smem()] + [vmem()] * (2 + len(prevs) + len(grads)),
        out_specs=(vmem(),) * 3,
        compiler_params=params(16),
        cost_estimate=cost(4 * tokens * tokens * width, 8 * tokens * width),
        name="query_products",
    )(place, ctx, key_rows, value_rows, *prevs, *grads)


def later_products(place, ctx, query_rows, key_rows, value_rows, grad_rows, near, far, nexts, sub):
    tokens, width = key_rows.shape
    return pl.pallas_call(
        functools.partial(later_body, sub, len(nexts)),
        out_shape=(jax.ShapeDtypeStruct((tokens, width), F32),) * 2
        + (jax.ShapeDtypeStruct((tokens, width), BF16),) * 2,
        in_specs=[smem(), smem()] + [vmem()] * (6 + len(nexts)),
        out_specs=(vmem(),) * 4,
        compiler_params=params(16),
        cost_estimate=cost(8 * tokens * tokens * width, 10 * tokens * width),
        name="later_products",
    )(place, ctx, query_rows, key_rows, value_rows, grad_rows, near, far, *nexts)


def end_body(sub, ctx_ref, half_ref, got_ref, key_ref, value_ref, grad_ref, *refs):
    part_refs, (out_refs, done, sems) = refs[:3], (refs[-5:-2], refs[-2], refs[-1])
    upper = ctx_ref[0] >= half_ref[0]
    lefts, dims = (grad_ref, value_ref, key_ref), (NT, NT, NN)

    def renew(which):
        copies = []
        for n in range(key_ref.shape[0] // sub):
            rows = slice(n * sub, (n + 1) * sub)
            for k in which:
                for h in range(got_ref.shape[0]):
                    cols = head_cols(h)
                    add = dot(lefts[k][rows, cols], got_ref[h], dims[k])
                    done[k, rows, cols] = (part_refs[k][rows, cols] + add).astype(BF16)
                copy = pltpu.make_async_copy(
                    done.at[k, pl.ds(n * sub, sub), :],
                    out_refs[k].at[pl.ds(n * sub, sub), :],
                    sems.at[k, n],
                )
                copy.start()
                copies.append(copy)
        for copy in copies:
            copy.wait()

    @pl.when(upper)
    def _():
        renew((0,))

    @pl.when(jnp.logical_not(upper))
    def _():
        renew((1, 2))


def end_products(ctx, half, got, key_rows, value_rows, grad_rows, parts, dones, sub):
    tokens, width = key_rows.shape
    return pl.pallas_call(
        functools.partial(end_body, sub),
        out_shape=(jax.ShapeDtypeStruct((tokens, width), BF16),) * 3,
        in_specs=[smem(), smem()] + [vmem()] * 7 + [hbm()] * 3,
        out_specs=(hbm(),) * 3,
        scratch_shapes=[
            pltpu.VMEM((3, tokens, width), BF16),
            pltpu.SemaphoreType.DMA((3, tokens // sub)),
        ],
        input_output_aliases={9 + k: k for k in range(3)},
        compiler_params=params(16),
        cost_estimate=cost(6 * tokens * width * HEAD_DIM, 16 * tokens * width),
        name="end_products",
    )(ctx, half, got, key_rows, value_rows, grad_rows, *parts, *dones)


def scan_states(wide, short, reverse, ties, name):
    size = lax.axis_size("ctx")
    send = lambda payload, pairs: lax.ppermute(payload, "ctx", pairs)
    received = [send(short, [(i, i ^ k) for i in range(size)]) for k in range(1, QUAD)]
    reach = QUAD
    while reach < size // 2:
        payload = group_state(wide, received, ties if reach == QUAD else [], "%s_%d" % (name, reach))
        if reverse:
            pairs = [(i + reach, i) for i in range(size - reach)]
        else:
            pairs = [(i, i + reach) for i in range(size - reach)]
        received.append(send(payload, pairs))
        reach *= 2
    return received


def per_device(out_grad, keep_mask, out_weight, query_rows, key_rows, value_rows):
    size = lax.axis_size("head")
    place = lax.axis_index("head").astype(jnp.int32).reshape(1)
    ctx = lax.axis_index("ctx").astype(jnp.int32).reshape(1)
    own_rows = out_grad.shape[0]
    half = jnp.full((1,), lax.axis_size("ctx") // 2, jnp.int32)
    unit = own_rows // 16
    split = 9 * unit

    def swap(array, distance):
        return lax.ppermute(array, "head", [(i, i ^ distance) for i in range(size)])

    first, *near_first = mask_rows(out_grad, keep_mask, 0, (5 * unit, 4 * unit), "mask_first")
    last, *near_last = mask_rows(out_grad, keep_mask, split, (4 * unit, 3 * unit), "mask_last")
    far_first, far_last = swap(first, 2), swap(last, 2)
    kv_wide, kv_short = kv_state(key_rows, value_rows)
    prevs = scan_states(kv_wide, kv_short, False, [], "prev")
    near = [swap(piece, 1) for piece in near_first + near_last]

    part = functools.partial(grad_part, place, query_rows, out_weight, own_rows)
    grads, places, states = [], [], []

    def run(befores, pieces, arrays, name, mib=20):
        got = part(befores, pieces, arrays, name, mib)
        at, spots = 0, []
        for (flip, row), array in zip(pieces, arrays):
            spots.append((at, array.shape[0], flip, row))
            at += array.shape[0]
        grads.append(got[0])
        places.append(tuple(spots))
        states.append(got[1])
        return got

    pieces = ((0, 0), (0, split), (1, 0), (1, 5 * unit), (1, split), (1, split + 4 * unit))
    run([], pieces, [first, last] + near, "grad_near", 60)

    prev_sum = group_state(kv_wide, prevs, [states[0]], "prev_sum")

    far_first = after(far_first, prev_sum, states[0])
    run([], ((2, 0), (3, 0)), [far_first, swap(far_first, 1)], "grad_far")
    _, far, wide, short = run(
        [states[1], states[0]],
        ((2, split), (3, split)),
        [far_last, swap(far_last, 1)],
        "grad_last",
    )

    spots = tuple(places)
    query_part, query_done, grad_rows = query_products(place, ctx, key_rows, value_rows, prevs, grads, spots, own_rows)
    nexts = scan_states(wide, short, True, [query_part], "next")
    nexts[-1] = after(nexts[-1], query_part)
    payload = swap_state(ctx, half, prev_sum, wide, nexts)
    size = lax.axis_size("ctx")
    got = lax.ppermute(payload, "ctx", [(i, (i + size // 2) % size) for i in range(size)])
    key_part, value_part, key_done, value_done = later_products(
        place, ctx, query_rows, key_rows, value_rows, grad_rows, states[0], far, nexts, own_rows
    )
    parts = (query_part, key_part, value_part)
    dones = (query_done, key_done, value_done)
    return end_products(ctx, half, got, key_rows, value_rows, grad_rows, parts, dones, own_rows // 2)


def solution(mesh):
    placed = (
        P(("ctx", "head"), None),
        P(("ctx", "head"), None),
        P("head", None),
        P("ctx", "head"),
        P("ctx", "head"),
        P("ctx", "head"),
    )
    return jax.shard_map(
        per_device,
        mesh=mesh,
        in_specs=placed,
        out_specs=(P("ctx", "head"), P("ctx", "head"), P("ctx", "head")),
        check_vma=False,
    )
```
